256 devices in a mesh: pts: 128 (over x, z, y), grp: 2 (over core).
Axes of the slice: x: 4, y: 4, z: 8, core: 2. Of those that a mesh axis runs over, the one named last changes fastest.
Arguments:
- features: bfloat16 [131072, 512], P('pts', 'grp'), may hold values from -6 to 6
- hilbert_rank: int32 [131072], P('pts'), may hold values from 0 to 131071, as said below
- trans_rank: int32 [131072], P('pts'), may hold values from 0 to 131071, as said below
- ln_gain: float32 [2, 512], replicated, may hold values from 0.1 to 1.9
- ln_bias: float32 [2, 512], replicated, may hold values from -3 to 3
- w_qkv: bfloat16 [2, 512, 3, 512], P(None, None, None, 'grp'), may hold values from -2 to 2
- w_proj: bfloat16 [2, 512, 512], P(None, 'grp'), may hold values from -1 to 1
Outputs:
- refined: bfloat16 [131072, 512], P('pts', 'grp')
The draws below stay inside these ranges and needn't reach their ends.
Inputs may be any that keep to these rules, and one draw needn't show every extreme that they name: `hilbert_rank`: a permutation of 0 to 131071; the points of one device's shard land on any one device (itself included) at most 12 times, and exactly 12 times for some pairs in every draw. `trans_rank`: a permutation of 0 to 131071; the points of one device's shard land on any one device (itself included) at most 12 times, and exactly 12 times for some pairs in every draw.
All inputs are finite; a program needn't handle non-finite values.
Results may differ from the reference program's by a relative error of at most 0.03.
The reference program's roundings to bfloat16 on the way (of `current`, `ordered`, `normed`, `projected`, `weights`, `attended` and `updated`) count: a program that leaves them out, or rounds other values in their place, can miss the bound.
Values may be sent and summed in bfloat16 or wider, within the bound.
No kernel may reach another device: no remote copies, remote signals or barrier semaphores. Data moves between devices by JAX's collectives and lax.ppermute only.
A program may use at most 64 MiB of HBM per device.

```python
import jax
import jax.numpy as jnp
from jax import lax

C = 512
HEADS = 32
HEAD = 16
PATCH = 512
BLOCKS = 2
PTS_DEV = 1024
TOTAL = 131072


def make_ranking(key):
    row_count = PTS_DEV
    peer_count = TOTAL // PTS_DEV
    block_rows = row_count // (2 * peer_count)
    block_count = 2 * peer_count
    keys = jax.random.split(key, 5)
    pairing = jax.random.permutation(keys[0], peer_count)
    tilting = jax.random.randint(keys[1], (peer_count // 2,), -1, 2).astype(jnp.int32)
    tilting = tilting.at[0].set(1)
    counting = jnp.zeros((peer_count,), jnp.int32)
    counting = counting.at[pairing[0::2]].set(2 + tilting).at[pairing[1::2]].set(2 - tilting)
    offsets = jnp.repeat(jnp.arange(peer_count, dtype=jnp.int32), counting, total_repeat_length=block_count)
    offsets = jax.random.permutation(keys[2], offsets)
    source_perm = jax.vmap(lambda sub: jax.random.permutation(sub, row_count))(jax.random.split(keys[3], peer_count))
    target_perm = jax.vmap(lambda sub: jax.random.permutation(sub, row_count))(jax.random.split(keys[4], peer_count))
    source_perm = source_perm.astype(jnp.int32)
    target_perm = target_perm.astype(jnp.int32)
    block_of = source_perm // block_rows
    within = source_perm % block_rows
    sources = jnp.arange(peer_count, dtype=jnp.int32)[:, None]
    target = (sources + offsets[block_of]) % peer_count
    slot_number = block_of * block_rows + within
    final = target_perm[target, slot_number]
    return (target * row_count + final).reshape(-1).astype(jnp.int32)


def draw_hilbert_rank(key, part):
    key = jax.random.fold_in(key, 3)
    return make_ranking(key)


def draw_trans_rank(key, part):
    key = jax.random.fold_in(key, 7)
    return make_ranking(key)


def draw_w_qkv(key, part):
    key = jax.random.fold_in(key, 11)
    key_main = jax.random.fold_in(key, 0)
    scaling = 1.5 * C ** (-0.5)
    base = jax.random.normal(key_main, (BLOCKS, C, 3, C), jnp.float32) * scaling
    return jnp.clip(base, -2.0, 2.0).astype(jnp.bfloat16)


def block_scale(stream_key, shape, shards, least, high):
    def one(position, shards_of):
        draws = jax.random.uniform(jax.random.fold_in(jax.random.fold_in(stream_key, 6), position), (shards_of,), jnp.float32, least / len(shards), high / len(shards))
        return jnp.repeat(jnp.exp(draws), shape[position] // shards_of).reshape((-1,) + (1,) * (len(shape) - position - 1))

    loudness = one(*shards[0])
    for cut in shards[1:]:
        loudness = loudness * one(*cut)
    return loudness


def scatter_about(rng, shape, spread, reach, shards=(), kind=jnp.bfloat16):
    values = jax.random.normal(rng, shape, jnp.float32) * spread
    if len(shards) > 0:
        values = block_scale(rng, shape, shards, -0.22, 0.18) * values
    return jnp.clip(values, min=-reach, max=reach).astype(kind)


def setup_inputs(seed: int = 0) -> dict:
    key_list = jax.random.split(jax.random.key(seed), 8)
    return {
        "features": scatter_about(key_list[0], (TOTAL, C), 1.0, 6.0, ((0, 128), (1, 2))),
        "hilbert_rank": draw_hilbert_rank(jax.random.fold_in(key_list[7], 71), 0),
        "trans_rank": draw_trans_rank(jax.random.fold_in(key_list[7], 71), 0),
        "ln_gain": jnp.clip(1.0 + 0.18 * jax.random.normal(key_list[3], (BLOCKS, C), jnp.float32), 0.1, 1.9),
        "ln_bias": scatter_about(key_list[4], (BLOCKS, C), 0.5, 3.0, (), jnp.float32),
        "w_qkv": draw_w_qkv(jax.random.fold_in(key_list[7], 71), 0),
        "w_proj": scatter_about(key_list[6], (BLOCKS, C, C), (C // 16) ** -0.5, 1.0, ((1, 2),)),
    }


epsilon = 1e-05

def layer_norm(stream, gain_row, bias_row):
    values_f = stream.astype(jnp.float32)
    full_width = stream.shape[1]
    average = lax.optimization_barrier(jnp.sum(values_f, axis=1)) / full_width
    variance = lax.optimization_barrier(jnp.sum(values_f * values_f, axis=1)) / full_width - average * average
    normed = (values_f - average[:, None]) * lax.rsqrt(variance + epsilon)[:, None] * gain_row + bias_row
    return normed.astype(jnp.bfloat16)

def attend_patch(triple):
    query_blk, key_blk, value_blk = triple
    scaling = HEAD ** (-0.5)
    scores = jnp.einsum('qhd,khd->hqk', query_blk.astype(jnp.float32), key_blk.astype(jnp.float32)) * scaling
    row_max = lax.optimization_barrier(jnp.max(scores, axis=2, keepdims=True))
    exponent = jnp.exp(scores - row_max)
    weights = (exponent / lax.optimization_barrier(jnp.sum(exponent, axis=2, keepdims=True))).astype(jnp.bfloat16)
    weights = lax.optimization_barrier(weights).astype(jnp.float32)
    attended = jnp.einsum('hqk,khd->qhd', weights, value_blk.astype(jnp.float32))
    return attended.astype(jnp.bfloat16)

def run_block(stream, gain_row, bias_row, qkv_weight, proj_weight):
    normed = layer_norm(stream, gain_row, bias_row)
    projected = jnp.dot(normed, qkv_weight.reshape(C, 3 * C), preferred_element_type=jnp.float32)
    projected = projected.astype(jnp.bfloat16).reshape(TOTAL, 3, C)

    def heads_of(column):
        return projected[:, column].reshape(TOTAL // PATCH, PATCH, HEADS, HEAD)
    attended = lax.map(attend_patch, (heads_of(0), heads_of(1), heads_of(2))).reshape(TOTAL, C)
    mixture = jnp.dot(attended, proj_weight, preferred_element_type=jnp.float32)
    return (stream.astype(jnp.float32) + mixture).astype(jnp.bfloat16)

def reference(features, hilbert_rank, trans_rank, ln_gain, ln_bias, w_qkv, w_proj):
    current = features
    for block_index, ranking in enumerate((hilbert_rank, trans_rank)):
        ordering = jnp.zeros((TOTAL,), jnp.int32).at[ranking].set(jnp.arange(TOTAL, dtype=jnp.int32))
        ordered = current[ordering]
        updated = run_block(ordered, ln_gain[block_index], ln_bias[block_index], w_qkv[block_index], w_proj[block_index])
        current = updated[ranking]
    return current
```

```python
import functools
import math

import jax
import jax.numpy as jnp
from jax import lax
from jax.experimental import pallas as pl
from jax.experimental.pallas import tpu as pltpu
from jax.sharding import PartitionSpec as P

ROWS = 1024
PEERS = 128
HALF = 256
FULL = 512
PATCH = 512
HEADS = 32
HEAD = 16
EPSILON = 1e-05
EXP_SCALE = HEAD ** (-0.5) * math.log2(math.e)
VMEM_BYTES = 48 * 2**20


f32 = jnp.float32
bf16 = jnp.bfloat16


def iota(shape, axis):
    return lax.broadcasted_iota(jnp.int32, shape, axis)


def dot(left, right):
    return jnp.dot(left, right, preferred_element_type=f32)


def onehot(mask):
    return jnp.where(mask, 1.0, 0.0).astype(bf16)


def slot_rows(rank_row):
    owner = lax.shift_right_logical(rank_row, 10)
    position = rank_row & (ROWS - 1)
    owners = onehot(iota((PEERS, ROWS), 0) == owner)
    earlier = onehot(iota((ROWS, ROWS), 0) < iota((ROWS, ROWS), 1))
    running = dot(owners, earlier)
    slot = jnp.sum(running * owners.astype(f32), axis=0, keepdims=True).astype(jnp.int32)
    low = jnp.where(slot < 8, owner * 8 + slot, -1)
    high = jnp.where((slot >= 8) & (slot < 12), owner * 8 + slot - 8, -1)
    return low, high, position


def pack(low_mask, high_mask, rows):
    low = dot(onehot(low_mask), rows)
    high = dot(onehot(high_mask), rows)
    first = (iota((ROWS, 128), 0) & 4) == 0
    return low, jnp.where(first, high[:, :128], high[:, 128:HALF]), high


def unpack(low_mask, first_mask, second_mask, message):
    tail = message[:, HALF:HALF + 128]
    low = dot(onehot(low_mask), message[:, :HALF])
    first = dot(onehot(first_mask), tail)
    second = dot(onehot(second_mask), tail)
    return jnp.concatenate([low[:, :128] + first, low[:, 128:] + second], axis=1)


def send_kernel(hilbert_ref, trans_ref, features_ref, message_ref, index_ref):
    features = features_ref[...]
    rows = iota((ROWS, ROWS), 0)
    rows_high = rows & ~4
    parts = []
    label_rows = []
    for rank_ref in (hilbert_ref, trans_ref):
        low, high, position = slot_rows(rank_ref[...])
        parts.append((low, high))
        label_rows.append(lax.shift_right_logical(position, 5) + 1)
        label_rows.append(position & 31)
    index_ref[...] = jnp.concatenate(
        [parts[0][0], parts[0][1], parts[1][0], parts[1][1]] + [jnp.full((4, ROWS), -1, jnp.int32)], axis=0
    )
    lanes = iota((ROWS, 128), 1)
    labels = jnp.concatenate(
        [row.astype(f32) for row in label_rows] + [jnp.zeros((124, ROWS), f32)], axis=0
    ).T

    def labels_at(source, target):
        columns = jnp.where(lanes == target, labels[:, source:source + 1], 0.0)
        return (columns + jnp.where(lanes == target + 1, labels[:, source + 1:source + 2], 0.0)).astype(bf16)

    low_mask = rows == parts[0][0]
    high_mask = rows_high == parts[0][1]
    low = dot(onehot(low_mask), jnp.concatenate([features, labels_at(0, 0)], axis=1))
    high = dot(onehot(high_mask), jnp.concatenate([features, labels_at(0, 2)], axis=1))
    first = (iota((ROWS, 128), 0) & 4) == 0
    message_ref[:, :HALF] = low[:, :HALF].astype(bf16)
    message_ref[:, HALF:384] = jnp.where(first, high[:, :128], high[:, 128:HALF]).astype(bf16)
    tile = low[:, HALF:] + high[:, HALF:]
    tile += dot(onehot(rows == parts[1][0]), labels_at(2, 4))
    tile += dot(onehot(rows_high == parts[1][1]), labels_at(2, 6))
    message_ref[:, 384:] = tile.astype(bf16)


def columns_of(labels, block):
    values = labels.astype(f32)[:, 4 * block:4 * block + 4].astype(jnp.int32)
    return (values[:, 0:1] - 1) * 32 + values[:, 1:2], (values[:, 2:3] - 1) * 32 + values[:, 3:4]


def place_kernel(base_ref, message_ref, labels_ref, out_ref, *, block):
    values = labels_ref[...].astype(f32).T[4 * block:4 * block + 4].astype(jnp.int32)
    low = (values[0:1] - 1) * 32 + values[1:2]
    high = (values[2:3] - 1) * 32 + values[3:4]
    first = (iota((1, ROWS), 1) & 4) == 0
    targets = iota((PATCH, ROWS), 0) + base_ref[0]
    out_ref[...] = unpack(
        targets == low,
        targets == jnp.where(first, high, -1),
        targets == jnp.where(first, -1, high),
        message_ref[:, :384],
    ).astype(bf16)


def return_kernel(core_ref, kept_ref, received_ref, labels_ref, out_ref, *, block):
    first = core_ref[0] == 0
    kept, received = kept_ref[...], received_ref[...]
    rows = jnp.concatenate([jnp.where(first, kept, received), jnp.where(first, received, kept)], axis=0)
    low, high = columns_of(labels_ref[...], block)
    targets = iota((ROWS, ROWS), 1)
    body, tail, _ = pack(targets == low, targets == high, rows)
    out_ref[:, :HALF] = body.astype(bf16)
    out_ref[:, HALF:] = tail.astype(bf16)


def home_rows(index, block, message):
    columns = index.astype(f32).T.astype(jnp.int32)
    low, high = columns[:, 2 * block:2 * block + 1], columns[:, 2 * block + 1:2 * block + 2]
    sources = iota((ROWS, ROWS), 1)
    return unpack(sources == low, sources == high, sources == jnp.where(high < 0, -1, high + 4), message)


def padded_index(index_ref):
    return jnp.concatenate([index_ref[...], jnp.full((120, ROWS), -1, jnp.int32)], axis=0)


def middle_kernel(index_ref, message_ref, out_ref):
    index = padded_index(index_ref)
    rows = home_rows(index, 0, message_ref[...]).astype(bf16)
    targets = iota((ROWS, ROWS), 0)
    body, tail, _ = pack(targets == index[2:3], (targets & ~4) == index[3:4], rows)
    out_ref[:, :HALF] = body.astype(bf16)
    out_ref[:, HALF:] = tail.astype(bf16)


def home_kernel(index_ref, message_ref, out_ref):
    out_ref[...] = home_rows(padded_index(index_ref), 1, message_ref[...]).astype(bf16)


def attention_kernel(
    core_ref, own_ref, other_ref, gain_ref, bias_ref, qkv_own_ref, qkv_other_ref, proj_own_ref, proj_other_ref,
    kept_ref, sent_ref, keys_s, queries_s, values_s, attended_s,
):
    first = core_ref[0] == 0
    own, other = own_ref[...], other_ref[...]
    ordered = jnp.concatenate([jnp.where(first, own, other), jnp.where(first, other, own)], axis=1)
    ordered = ordered.astype(f32)
    average = jnp.sum(ordered, axis=1, keepdims=True) / FULL
    variance = jnp.sum(ordered * ordered, axis=1, keepdims=True) / FULL - average * average
    normed = ((ordered - average) * lax.rsqrt(variance + EPSILON) * gain_ref[...] + bias_ref[...]).astype(bf16)
    lane = iota((PATCH, 128), 1)
    for part, weight_ref in enumerate((qkv_own_ref, qkv_other_ref)):
        queries = dot(normed, weight_ref[:, :HALF])
        keys = dot(normed, weight_ref[:, HALF:2 * HALF]).astype(bf16)
        values = dot(normed, weight_ref[:, 2 * HALF:])
        queries_s[part * HALF:(part + 1) * HALF, :] = queries.T.astype(bf16)
        values_s[part * HALF:(part + 1) * HALF, :] = values.T.astype(bf16)
        for group in range(2):
            keys_g = keys[:, group * 128:(group + 1) * 128]
            for head in range(8):
                keys_s[part * 16 + group * 8 + head] = jnp.where(lane // HEAD == head, keys_g, jnp.zeros_like(keys_g))

    def one_head(head):
        channels = pl.ds(pl.multiple_of(head * HEAD, HEAD), HEAD)
        group = pl.ds(pl.multiple_of(head // 8 * 128, 128), 128)
        scores = dot(keys_s[head], queries_s[group, :])
        row_max = jnp.max(scores, axis=0, keepdims=True)
        exponent = jnp.exp2((scores - row_max) * EXP_SCALE)
        weights = (exponent * (1.0 / jnp.sum(exponent, axis=0, keepdims=True))).astype(bf16)
        attended_s[channels, :] = dot(values_s[channels, :], weights).astype(bf16)

    def two_heads(step, carry):
        one_head(step * 2)
        one_head(step * 2 + 1)
        return carry

    lax.fori_loop(0, HEADS // 2, two_heads, 0)
    attended = attended_s[...].astype(f32).T.astype(bf16)
    mixture = dot(attended[:, :HALF], proj_own_ref[...]) + dot(attended[:, HALF:], proj_other_ref[...])
    updated = (ordered + mixture).astype(bf16)
    kept_ref[...] = jnp.where(first, updated[:, :HALF], updated[:, HALF:])
    sent_ref[...] = jnp.where(first, updated[:, HALF:], updated[:, :HALF])


def call(kernel, name, outs, *args, scalars=0, scratch=(), flops=10**9):
    vmem = pl.BlockSpec(memory_space=pltpu.VMEM)
    smem = pl.BlockSpec(memory_space=pltpu.SMEM)
    specs = [smem] * scalars + [vmem] * (len(args) - scalars)
    many = isinstance(outs, list)
    return pl.pallas_call(
        kernel,
        out_shape=outs,
        in_specs=specs,
        out_specs=[vmem] * len(outs) if many else vmem,
        scratch_shapes=list(scratch),
        compiler_params=pltpu.CompilerParams(vmem_limit_bytes=VMEM_BYTES),
        cost_estimate=pl.CostEstimate(flops=flops, bytes_accessed=2 * 2**20, transcendentals=0),
        name=name,
    )(*args)


def shape(*dims, dtype=bf16):
    return jax.ShapeDtypeStruct(dims, dtype)


def exchange(message):
    width = message.shape[1]
    blocks = message.reshape(PEERS, ROWS // PEERS, width)
    return lax.all_to_all(blocks, "pts", split_axis=0, concat_axis=0, tiled=True).reshape(ROWS, width)


def swap(array):
    return lax.ppermute(array, "grp", [(0, 1), (1, 0)])


def block(index, core, message, labels, gain, bias, qkv_own, qkv_other, proj_own, proj_other):
    place = functools.partial(place_kernel, block=index)
    mine = (core * PATCH).reshape(1)
    theirs = ((1 - core) * PATCH).reshape(1)
    part = shape(PATCH, HALF)
    leaving = call(place, "place_other", part, theirs, message, labels, scalars=1)
    other = swap(leaving)
    own = call(place, "place_own", part, mine, message, labels, scalars=1)
    core = core.reshape(1)
    kept, sent = call(
        attention_kernel, "attention", [part, part], core, own, other, gain, bias, qkv_own, qkv_other, proj_own,
        proj_other, scalars=1,
        scratch=[pltpu.VMEM((HEADS, PATCH, 128), bf16)] + [pltpu.VMEM((FULL, PATCH), bf16)] * 3, flops=2 * 10**10,
    )
    received = swap(sent)
    back = functools.partial(return_kernel, block=index)
    return exchange(call(back, "return", shape(ROWS, 384), core, kept, received, labels, scalars=1))


def local(features, hilbert_rank, trans_rank, ln_gain, ln_bias, w_qkv, w_proj):
    core = lax.axis_index("grp").astype(jnp.int32)
    qkv = w_qkv.reshape(2, FULL, 3 * HALF)
    qkv_other, proj_other = swap(qkv), swap(w_proj)
    message, index = call(
        send_kernel, "send", [shape(ROWS, 512), shape(8, ROWS, dtype=jnp.int32)],
        hilbert_rank.reshape(1, ROWS), trans_rank.reshape(1, ROWS), features,
    )
    arrived = exchange(message)
    labels = arrived[:, 384:]

    def run(number, data):
        return block(
            number, core, data, labels, ln_gain[number:number + 1], ln_bias[number:number + 1],
            qkv[number], qkv_other[number], w_proj[number], proj_other[number],
        )

    landed = run(0, arrived)
    landed = run(1, exchange(call(middle_kernel, "middle", shape(ROWS, 384), index, landed)))
    return call(home_kernel, "home", shape(ROWS, HALF), index, landed)


def solution(mesh):
    in_specs = (
        P("pts", "grp"),
        P("pts"),
        P("pts"),
        P(),
        P(),
        P(None, None, None, "grp"),
        P(None, "grp", None),
    )
    return jax.shard_map(local, mesh=mesh, in_specs=in_specs, out_specs=P("pts", "grp"), check_vma=False)
```

```python
import functools
import math

import jax
import jax.numpy as jnp
from jax import lax
from jax.experimental import pallas as pl
from jax.experimental.pallas import tpu as pltpu
from jax.sharding import PartitionSpec as P

ROWS = 1024
PEERS = 128
HALF = 256
FULL = 512
PATCH = 512
HEADS = 32
HEAD = 16
EPSILON = 1e-05
EXP_SCALE = HEAD ** (-0.5) * math.log2(math.e)
CHUNK = 128
VMEM_BYTES = 48 * 2**20


f32 = jnp.float32
bf16 = jnp.bfloat16


def iota(shape, axis):
    return lax.broadcasted_iota(jnp.int32, shape, axis)


def dot(left, right):
    return jnp.dot(left, right, preferred_element_type=f32)


def onehot(mask):
    return jnp.where(mask, 1.0, 0.0).astype(bf16)


def slot_rows(rank_row):
    owner = lax.shift_right_logical(rank_row, 10)
    position = rank_row & (ROWS - 1)
    owners = onehot(iota((PEERS, ROWS), 0) == owner)
    earlier = onehot(iota((ROWS, ROWS), 0) < iota((ROWS, ROWS), 1))
    running = dot(owners, earlier)
    slot = jnp.sum(running * owners.astype(f32), axis=0, keepdims=True).astype(jnp.int32)
    low = jnp.where(slot < 8, owner * 8 + slot, -1)
    high = jnp.where((slot >= 8) & (slot < 12), owner * 8 + slot - 8, -1)
    return low, high, position


def pack(low_mask, high_mask, rows):
    low = dot(onehot(low_mask), rows)
    high = dot(onehot(high_mask), rows)
    first = (iota((ROWS, 128), 0) & 4) == 0
    return low, jnp.where(first, high[:, :128], high[:, 128:HALF]), high


def unpack(low_mask, first_mask, second_mask, message):
    tail = message[:, HALF:HALF + 128]
    low = dot(onehot(low_mask), message[:, :HALF])
    first = dot(onehot(first_mask), tail)
    second = dot(onehot(second_mask), tail)
    return jnp.concatenate([low[:, :128] + first, low[:, 128:] + second], axis=1)


def send_kernel(hilbert_ref, trans_ref, features_ref, message_ref, index_ref):
    features = features_ref[...]
    rows = iota((ROWS, ROWS), 0)
    rows_high = rows & ~4
    parts = []
    label_rows = []
    for rank_ref in (hilbert_ref, trans_ref):
        low, high, position = slot_rows(rank_ref[...])
        parts.append((low, high))
        label_rows.append(lax.shift_right_logical(position, 5) + 1)
        label_rows.append(position & 31)
    index_ref[...] = jnp.concatenate(
        [parts[0][0], parts[0][1], parts[1][0], parts[1][1]] + [jnp.full((4, ROWS), -1, jnp.int32)], axis=0
    )
    lanes = iota((ROWS, 128), 1)
    labels = jnp.concatenate(
        [row.astype(f32) for row in label_rows] + [jnp.zeros((124, ROWS), f32)], axis=0
    ).T

    def labels_at(source, target):
        columns = jnp.where(lanes == target, labels[:, source:source + 1], 0.0)
        return (columns + jnp.where(lanes == target + 1, labels[:, source + 1:source + 2], 0.0)).astype(bf16)

    low_mask = rows == parts[0][0]
    high_mask = rows_high == parts[0][1]
    low = dot(onehot(low_mask), jnp.concatenate([features, labels_at(0, 0)], axis=1))
    high = dot(onehot(high_mask), jnp.concatenate([features, labels_at(0, 2)], axis=1))
    first = (iota((ROWS, 128), 0) & 4) == 0
    message_ref[:, :HALF] = low[:, :HALF].astype(bf16)
    message_ref[:, HALF:384] = jnp.where(first, high[:, :128], high[:, 128:HALF]).astype(bf16)
    tile = low[:, HALF:] + high[:, HALF:]
    tile += dot(onehot(rows == parts[1][0]), labels_at(2, 4))
    tile += dot(onehot(rows_high == parts[1][1]), labels_at(2, 6))
    message_ref[:, 384:] = tile.astype(bf16)


def columns_of(labels, block):
    values = labels.astype(f32)[:, 4 * block:4 * block + 4].astype(jnp.int32)
    return (values[:, 0:1] - 1) * 32 + values[:, 1:2], (values[:, 2:3] - 1) * 32 + values[:, 3:4]


def place_kernel(base_ref, message_ref, labels_ref, out_ref, *, block):
    values = labels_ref[...].astype(f32).T[4 * block:4 * block + 4].astype(jnp.int32)
    low = (values[0:1] - 1) * 32 + values[1:2]
    high = (values[2:3] - 1) * 32 + values[3:4]
    first = (iota((1, ROWS), 1) & 4) == 0
    targets = iota((PATCH, ROWS), 0) + base_ref[0]
    out_ref[...] = unpack(
        targets == low,
        targets == jnp.where(first, high, -1),
        targets == jnp.where(first, -1, high),
        message_ref[:, :384],
    ).astype(bf16)


def return_kernel(core_ref, kept_ref, received_ref, labels_ref, out_ref, *, block):
    first = core_ref[0] == 0
    kept, received = kept_ref[...], received_ref[...]
    rows = jnp.concatenate([jnp.where(first, kept, received), jnp.where(first, received, kept)], axis=0)
    low, high = columns_of(labels_ref[...], block)
    targets = iota((ROWS, ROWS), 1)
    body, tail, _ = pack(targets == low, targets == high, rows)
    out_ref[:, :HALF] = body.astype(bf16)
    out_ref[:, HALF:] = tail.astype(bf16)


def home_rows(index, block, message):
    columns = index.astype(f32).T.astype(jnp.int32)
    low, high = columns[:, 2 * block:2 * block + 1], columns[:, 2 * block + 1:2 * block + 2]
    sources = iota((ROWS, ROWS), 1)
    return unpack(sources == low, sources == high, sources == jnp.where(high < 0, -1, high + 4), message)


def padded_index(index_ref):
    return jnp.concatenate([index_ref[...], jnp.full((120, ROWS), -1, jnp.int32)], axis=0)


def middle_kernel(index_ref, message_ref, out_ref):
    index = padded_index(index_ref)
    rows = home_rows(index, 0, message_ref[...]).astype(bf16)
    targets = iota((ROWS, ROWS), 0)
    body, tail, _ = pack(targets == index[2:3], (targets & ~4) == index[3:4], rows)
    out_ref[:, :HALF] = body.astype(bf16)
    out_ref[:, HALF:] = tail.astype(bf16)


def home_kernel(index_ref, message_ref, out_ref):
    out_ref[...] = home_rows(padded_index(index_ref), 1, message_ref[...]).astype(bf16)


def attention_kernel(
    core_ref, own_ref, other_ref, gain_ref, bias_ref, qkv_own_ref, qkv_other_ref, proj_own_ref, proj_other_ref,
    kept_ref, sent_ref, keys_s, queries_s, values_s, attended_s, scores_a, scores_b, exponent_a, exponent_b, *, block,
):
    first = core_ref[0] == 0
    own, other = own_ref[...], other_ref[...]
    ordered = jnp.concatenate([jnp.where(first, own, other), jnp.where(first, other, own)], axis=1)
    ordered = ordered.astype(f32)
    average = jnp.sum(ordered, axis=1, keepdims=True) / FULL
    variance = jnp.sum(ordered * ordered, axis=1, keepdims=True) / FULL - average * average
    normed = (ordered - average) * lax.rsqrt(variance + EPSILON) * gain_ref[block:block + 1] + bias_ref[block:block + 1]
    normed = normed.astype(bf16)
    lane = iota((PATCH, 128), 1)
    for part, weight_ref in enumerate((qkv_own_ref, qkv_other_ref)):
        channels = slice(part * HALF, (part + 1) * HALF)
        queries_s[channels, :] = dot(normed, weight_ref[0]).T.astype(bf16)
        values_s[channels, :] = dot(normed, weight_ref[2]).T.astype(bf16)
        keys = dot(normed, weight_ref[1]).astype(bf16)
        for group in range(2):
            keys_g = keys[:, group * 128:(group + 1) * 128]
            for head in range(8):
                keys_s[part * 16 + group * 8 + head] = jnp.where(lane // HEAD == head, keys_g, jnp.zeros_like(keys_g))

    def channels_of(head):
        return pl.ds(pl.multiple_of(head * HEAD, HEAD), HEAD)

    def fold(array, reduction):
        return reduction(array.reshape(array.shape[0] // 8, 8, array.shape[1]), axis=0)

    def stage(scoring, exping, mixing, scores_to, scores_from, exponent_to, exponent_from, row_max, total):
        inverse = 1.0 / total
        new_max = jnp.full((8, PATCH), -jnp.inf, f32)
        new_total = jnp.zeros((8, PATCH), f32)
        attended = jnp.zeros((HEAD, PATCH), f32)
        for start in range(0, PATCH, CHUNK):
            part = slice(start, start + CHUNK)
            if scoring is not None:
                group = pl.ds(pl.multiple_of(scoring // 8 * 128, 128), 128)
                scores = dot(keys_s[scoring, part, :], queries_s[group, :])
                scores_to[part, :] = scores
                new_max = jnp.maximum(new_max, fold(scores, jnp.max))
            if exping is not None:
                exponent = jnp.exp2((scores_from[part, :] - row_max) * EXP_SCALE)
                exponent_to[part, :] = exponent
                new_total = new_total + fold(exponent, jnp.sum)
            if mixing is not None:
                weights = (exponent_from[part, :] * inverse).astype(bf16)
                attended = attended + dot(values_s[channels_of(mixing), part], weights)
        if mixing is not None:
            attended_s[channels_of(mixing), :] = attended.astype(bf16)
        return jnp.max(new_max, axis=0, keepdims=True), jnp.sum(new_total, axis=0, keepdims=True)

    def two_stages(step, carry):
        head = 2 * step
        carry = stage(head + 2, head + 1, head, scores_a, scores_b, exponent_b, exponent_a, *carry)
        return stage(head + 3, head + 2, head + 1, scores_b, scores_a, exponent_a, exponent_b, *carry)

    one = jnp.ones((1, PATCH), f32)
    row_max, _ = stage(0, None, None, scores_a, None, None, None, one, one)
    carry = stage(1, 0, None, scores_b, scores_a, exponent_a, None, row_max, one)
    carry = lax.fori_loop(0, HEADS // 2 - 1, two_stages, carry)
    carry = stage(None, HEADS - 1, HEADS - 2, None, scores_b, exponent_b, exponent_a, *carry)
    stage(None, None, HEADS - 1, None, None, None, exponent_b, one, carry[1])
    attended = attended_s[...].astype(f32).T.astype(bf16)
    mixture = dot(attended[:, :HALF], proj_own_ref[...]) + dot(attended[:, HALF:], proj_other_ref[...])
    updated = (ordered + mixture).astype(bf16)
    kept_ref[...] = jnp.where(first, updated[:, :HALF], updated[:, HALF:])
    sent_ref[...] = jnp.where(first, updated[:, HALF:], updated[:, :HALF])


def call(kernel, name, outs, *args, scalars=0, blocks={}, scratch=(), flops=10**9):
    vmem = pl.BlockSpec(memory_space=pltpu.VMEM)
    smem = pl.BlockSpec(memory_space=pltpu.SMEM)
    specs = [smem] * scalars + [vmem] * (len(args) - scalars)
    for number, (dims, index) in blocks.items():
        specs[number] = pl.BlockSpec(dims, functools.partial(lambda place, step: place, index), memory_space=pltpu.VMEM)
    many = isinstance(outs, list)
    return pl.pallas_call(
        kernel,
        grid=(1,),
        out_shape=outs,
        in_specs=specs,
        out_specs=[vmem] * len(outs) if many else vmem,
        scratch_shapes=list(scratch),
        compiler_params=pltpu.CompilerParams(vmem_limit_bytes=VMEM_BYTES),
        cost_estimate=pl.CostEstimate(flops=flops, bytes_accessed=2 * 2**20, transcendentals=0),
        name=name,
    )(*args)


def shape(*dims, dtype=bf16):
    return jax.ShapeDtypeStruct(dims, dtype)


def exchange(message):
    width = message.shape[1]
    blocks = message.reshape(PEERS, ROWS // PEERS, width)
    return lax.all_to_all(blocks, "pts", split_axis=0, concat_axis=0, tiled=True).reshape(ROWS, width)


def swap(array):
    return lax.ppermute(array, "grp", [(0, 1), (1, 0)])


def run_block(number, core, message, arrived, gain, bias, qkv_own, qkv_other, proj_own, proj_other):
    place = functools.partial(place_kernel, block=number)
    mine = (core * PATCH).reshape(1)
    theirs = ((1 - core) * PATCH).reshape(1)
    part = shape(PATCH, HALF)
    slots = ((ROWS, 384), (0, 0))
    labels = ((ROWS, 128), (0, 3))
    leaving = call(place, "place_other", part, theirs, message, arrived, scalars=1, blocks={1: slots, 2: labels})
    other = swap(leaving)
    own = call(place, "place_own", part, mine, message, arrived, scalars=1, blocks={1: slots, 2: labels})
    core = core.reshape(1)
    qkv_block = ((None, 3, FULL, HALF), (number, 0, 0, 0))
    proj_block = ((None, HALF, FULL), (number, 0, 0))
    kept, sent = call(
        functools.partial(attention_kernel, block=number), "attention", [part, part],
        core, own, other, gain, bias, qkv_own, qkv_other, proj_own, proj_other,
        scalars=1, blocks={5: qkv_block, 6: qkv_block, 7: proj_block, 8: proj_block},
        scratch=[pltpu.VMEM((HEADS, PATCH, 128), bf16)] + [pltpu.VMEM((FULL, PATCH), bf16)] * 3
        + [pltpu.VMEM((PATCH, PATCH), f32)] * 4, flops=2 * 10**10,
    )
    received = swap(sent)
    back = functools.partial(return_kernel, block=number)
    return exchange(
        call(back, "return", shape(ROWS, 384), core, kept, received, arrived, scalars=1, blocks={3: labels})
    )


def local(features, hilbert_rank, trans_rank, ln_gain, ln_bias, w_qkv, w_proj):
    core = lax.axis_index("grp").astype(jnp.int32)
    qkv = w_qkv.transpose(0, 2, 1, 3)
    qkv_other, proj_other = swap(qkv), swap(w_proj)
    message, index = call(
        send_kernel, "send", [shape(ROWS, 512), shape(8, ROWS, dtype=jnp.int32)],
        hilbert_rank.reshape(1, ROWS), trans_rank.reshape(1, ROWS), features,
    )
    arrived = exchange(message)
    weights = (ln_gain, ln_bias, qkv, qkv_other, w_proj, proj_other)
    landed = run_block(0, core, arrived, arrived, *weights)
    message = exchange(call(middle_kernel, "middle", shape(ROWS, 384), index, landed))
    landed = run_block(1, core, message, arrived, *weights)
    return call(home_kernel, "home", shape(ROWS, HALF), index, landed)


def solution(mesh):
    in_specs = (
        P("pts", "grp"),
        P("pts"),
        P("pts"),
        P(),
        P(),
        P(None, None, None, "grp"),
        P(None, "grp", None),
    )
    return jax.shard_map(local, mesh=mesh, in_specs=in_specs, out_specs=P("pts", "grp"), check_vma=False)
```

```python
import functools
import math

import jax
import jax.numpy as jnp
from jax import lax
from jax.experimental import pallas as pl
from jax.experimental.pallas import tpu as pltpu
from jax.sharding import PartitionSpec as P

ROWS = 1024
PEERS = 128
HALF = 256
FULL = 512
PATCH = 512
HEADS = 32
HEAD = 16
EPSILON = 1e-05
EXP_SCALE = HEAD ** (-0.5) * math.log2(math.e)
CHUNK = 128
VMEM_BYTES = 24 * 2**20
MOST_VMEM = 60 * 2**20

DIRECT = 24


f32 = jnp.float32
bf16 = jnp.bfloat16


def iota(shape, axis):
    return lax.broadcasted_iota(jnp.int32, shape, axis)


def dot(left, right):
    return jnp.dot(left, right, preferred_element_type=f32)


def onehot(mask):
    return jnp.where(mask, 1.0, 0.0).astype(bf16)


def integers(array):
    return array.astype(jnp.int32)


def earlier_peers(owner, earlier):
    owners = onehot(iota((PEERS, ROWS), 0) == owner)
    running = dot(owners, earlier)
    return owners, integers(jnp.sum(running * owners.astype(f32), axis=0, keepdims=True))


def before():
    return onehot(iota((ROWS, ROWS), 0) < iota((ROWS, ROWS), 1))


def pack(low_mask, high_mask, rows, out_ref):
    out_ref[:, :HALF] = dot(onehot(low_mask), rows).astype(bf16)
    high = dot(onehot(high_mask), rows)
    first = (iota((ROWS, 128), 0) & 4) == 0
    out_ref[:, HALF:384] = jnp.where(first, high[:, :128], high[:, 128:]).astype(bf16)


def unpack(low_mask, high_mask, message, low_more=(), high_more=()):
    tail = message[:, HALF:384].astype(f32)
    both = [tail.astype(bf16), pltpu.roll(tail, ROWS - 4, 0).astype(bf16)]
    low = dot(onehot(low_mask), jnp.concatenate([message[:, :HALF], *low_more], axis=1))
    return low + dot(onehot(high_mask), jnp.concatenate([*both, *high_more], axis=1))


def send_kernel(hilbert_ref, trans_ref, features_ref, message_ref, index_ref):
    features = features_ref[...]
    earlier = before()
    ranks = [hilbert_ref[...], trans_ref[...]]
    owners = [lax.shift_right_logical(rank, 10) for rank in ranks]
    highs = [lax.shift_right_logical(rank, 5) & 31 for rank in ranks]
    lows = [rank & 31 for rank in ranks]
    values = [[highs[0] + 1, lows[0], owners[1], highs[1], lows[1]], [highs[1] + 1, lows[1], owners[0]]]
    steps = iota((16, ROWS), 0)
    labels = jnp.zeros((PEERS, 128), f32)
    index = []
    for order in range(2):
        peers, slot = earlier_peers(owners[order], earlier)
        index.append(jnp.where(slot < 8, owners[order] * 8 + slot, -1))
        index.append(jnp.where((slot >= 8) & (slot < 12), owners[order] * 8 + slot - 8, -1))
        here = steps == slot
        spread = jnp.concatenate(
            [jnp.where(here, value, 0).astype(f32).astype(bf16) for value in values[order]], axis=0
        )
        empty = [jnp.zeros((16 * (8 - len(values[order])), ROWS), bf16)]
        spread = jnp.concatenate([spread] + empty if order == 0 else empty + [spread], axis=0)
        labels += lax.dot_general(peers, spread, (((1,), (1,)), ((), ())), preferred_element_type=f32)
    index_ref[...] = jnp.concatenate(index + [jnp.full((4, ROWS), -1, jnp.int32)], axis=0)
    rows = iota((ROWS, ROWS), 0)
    pack(rows == index[0], (rows & ~4) == index[1], features, message_ref)
    labels = jnp.broadcast_to(labels[:, None, :], (PEERS, 8, 128)).reshape(ROWS, 128)
    message_ref[:, 384:] = labels.astype(bf16)


def decode(labels):
    labels = labels.astype(f32)
    row, lane = iota((ROWS, 128), 0), iota((ROWS, 128), 1)
    low = jnp.where((lane & 15) == (row & 7), labels, 0.0).astype(bf16)
    high = jnp.where((lane & 15) == 8 + (row & 3), labels, 0.0).astype(bf16)
    value, column = iota((128, 128), 0) // 16, iota((128, 128), 1)

    def table(entries):
        weights = jnp.zeros((128, 128), f32)
        for to, source, weight in entries:
            weights += jnp.where((column == to) & (value == source), float(weight), 0.0)
        return weights.astype(bf16)

    entries = [(0, 0, 32), (0, 1, 1), (2, 2, 1024), (2, 3, 32), (2, 4, 1), (4, 5, 32), (4, 6, 1), (6, 7, 1)]
    codes = dot(low, table(entries)) + dot(high, table([(to + 1, v, w) for to, v, w in entries]))
    codes -= jnp.where((lane < 2) | (lane == 4) | (lane == 5), 32.0, 0.0)
    parts = table([(0, 2, 1), (1, 3, 1), (2, 4, 1), (3, 7, 1)])
    return codes, dot(low, parts).astype(bf16), dot(high, parts).astype(bf16)


def position_masks(rows, order, targets):
    low, high = rows[4 * order:4 * order + 1], rows[4 * order + 1:4 * order + 2]
    return targets == low, targets == jnp.where((iota((1, ROWS), 1) & 4) == 0, high, -1)


def place_rows(base_ref, message_ref, rows, low_parts, high_parts, out_ref, ranks_ref):
    masks = position_masks(rows, 0, iota((PATCH, ROWS), 0) + base_ref[0])
    placed = unpack(*masks, message_ref[...], [low_parts], [high_parts])
    out_ref[...] = placed[:, :HALF].astype(bf16)
    ranks_ref[...] = placed[:, HALF:]


def decode_place_kernel(base_ref, message_ref, labels_ref, out_ref, ranks_ref, rows_ref, columns_ref, parts_ref):
    codes, low_parts, high_parts = decode(labels_ref[...])
    codes = integers(codes)
    rows = codes.T[:8]
    rows_ref[...], columns_ref[...] = rows, codes
    parts_ref[:, :128], parts_ref[:, 128:] = low_parts, high_parts
    place_rows(base_ref, message_ref, rows, low_parts, high_parts, out_ref, ranks_ref)


def place_kernel(base_ref, message_ref, rows_ref, parts_ref, out_ref, ranks_ref):
    place_rows(base_ref, message_ref, rows_ref[...], parts_ref[:, :128], parts_ref[:, 128:], out_ref, ranks_ref)


def place_second_kernel(base_ref, message_ref, rows_ref, out_ref):
    masks = position_masks(rows_ref[...], 1, iota((PATCH, ROWS), 0) + base_ref[0])
    out_ref[...] = unpack(*masks, message_ref[...]).astype(bf16)


def in_order(core_ref, own, other):
    first = core_ref[0] == 0
    return jnp.concatenate([jnp.where(first, own, other), jnp.where(first, other, own)], axis=0)


def return_kernel(core_ref, kept_ref, received_ref, codes_ref, out_ref, *, order):
    rows = in_order(core_ref, kept_ref[...], received_ref[...])
    codes = codes_ref[...]
    targets = iota((ROWS, ROWS), 1)
    low, high = 4 * order, 4 * order + 1
    pack(targets == codes[:, low:low + 1], targets == codes[:, high:high + 1], rows, out_ref)


def home_rows(index_ref, order, message):
    index = jnp.concatenate([index_ref[...], jnp.full((120, ROWS), -1, jnp.int32)], axis=0)
    columns = integers(index.astype(f32).T)
    sources = iota((ROWS, ROWS), 1)
    low, high = 2 * order, 2 * order + 1
    return unpack(sources == columns[:, low:low + 1], sources == columns[:, high:high + 1], message).astype(bf16)


def middle_kernel(index_ref, message_ref, out_ref):
    rows = home_rows(index_ref, 0, message_ref[...])
    targets = iota((ROWS, ROWS), 0)
    pack(targets == index_ref[2:3], (targets & ~4) == index_ref[3:4], rows, out_ref)


def home_kernel(index_ref, message_ref, out_ref):
    out_ref[...] = home_rows(index_ref, 1, message_ref[...])


def direct_index(owner, slot):
    row = owner * 8 + (slot & 7)
    return [jnp.where(lax.shift_right_logical(slot, 3) == third, row, -1) for third in range(DIRECT // 8)]


def leave_kernel(core_ref, own_ref, other_ref, index_ref, most_ref):
    parts = in_order(core_ref, own_ref[...], other_ref[...])
    parts_t = parts.T
    rank = integers(parts[:, 0:1] * 1024.0 + parts[:, 1:2] * 32.0 + parts[:, 2:3])
    owner = integers(parts_t[0:1])
    rank_t = owner * 1024 + integers(parts_t[1:2] * 32.0 + parts_t[2:3])
    ahead = (rank >= owner * 1024) & (rank < rank_t)
    slot = integers(jnp.sum(jnp.where(ahead, 1.0, 0.0), axis=0, keepdims=True))
    index_ref[...] = jnp.concatenate(direct_index(owner, slot) + [jnp.full((5, ROWS), -1, jnp.int32)], axis=0)
    most = jnp.max(slot.astype(f32), axis=1, keepdims=True) + 1.0
    most_ref[...] = jnp.broadcast_to(most, (1, 128))


def direct_kernel(core_ref, kept_ref, received_ref, index_ref, most_ref, out_ref):
    rows = in_order(core_ref, kept_ref[...], received_ref[...])
    targets = iota((ROWS, ROWS), 0)
    for third in range(DIRECT // 8):
        columns = slice(third * HALF, (third + 1) * HALF)
        packed = dot(onehot(targets == index_ref[third:third + 1]), rows)
        if third == 0:
            packed = jnp.where(most_ref[:, :1] > DIRECT, jnp.inf, packed)
        out_ref[:, columns] = packed.astype(bf16)


def arrive_kernel(rows_ref, parts_ref, index_ref):
    low, high = position_masks(rows_ref[...], 1, iota((ROWS, ROWS), 0))
    owner = dot(onehot(low), parts_ref[:, :128]) + dot(onehot(high), parts_ref[:, 128:])
    owner = integers(owner.T[3:4])
    _, slot = earlier_peers(owner, before())
    index = direct_index(owner, slot) + [jnp.full((125, ROWS), -1, jnp.int32)]
    index_ref[...] = integers(jnp.concatenate(index, axis=0).astype(f32).T)


def place_direct_kernel(base_ref, index_ref, message_ref, out_ref, *full_ref):
    if full_ref:
        largest = jnp.max(jnp.abs(message_ref[:, :128].astype(f32)))
        full_ref[0][0, 0] = jnp.where(largest == jnp.inf, 1, 0)
    index = index_ref[pl.ds(pl.multiple_of(base_ref[0], PATCH), PATCH), :]
    sources = iota((PATCH, ROWS), 1)
    placed = jnp.zeros((PATCH, HALF), f32)
    for third in range(DIRECT // 8):
        mask = sources == index[:, third:third + 1]
        placed += dot(onehot(mask), message_ref[:, third * HALF:(third + 1) * HALF])
    out_ref[...] = placed.astype(bf16)


def attention_kernel(
    core_ref, own_ref, other_ref, gain_ref, bias_ref, qkv_own_ref, qkv_other_ref, proj_own_ref, proj_other_ref,
    kept_ref, sent_ref, keys_s, queries_s, values_s, attended_s, scores_a, scores_b, exponent_a, exponent_b, *, block,
):
    first = core_ref[0] == 0
    own, other = own_ref[...], other_ref[...]
    ordered = jnp.concatenate([jnp.where(first, own, other), jnp.where(first, other, own)], axis=1)
    ordered = ordered.astype(f32)
    average = jnp.sum(ordered, axis=1, keepdims=True) / FULL
    variance = jnp.sum(ordered * ordered, axis=1, keepdims=True) / FULL - average * average
    normed = (ordered - average) * lax.rsqrt(variance + EPSILON) * gain_ref[block:block + 1] + bias_ref[block:block + 1]
    normed = normed.astype(bf16)
    lane = iota((PATCH, 128), 1)
    for part, weight_ref in enumerate((qkv_own_ref, qkv_other_ref)):
        channels = slice(part * HALF, (part + 1) * HALF)
        queries_s[channels, :] = dot(normed, weight_ref[0]).T.astype(bf16)
        values_s[channels, :] = dot(normed, weight_ref[2]).T.astype(bf16)
        keys = dot(normed, weight_ref[1]).astype(bf16)
        for group in range(2):
            keys_g = keys[:, group * 128:(group + 1) * 128]
            for head in range(8):
                keys_s[part * 16 + group * 8 + head] = jnp.where(lane // HEAD == head, keys_g, jnp.zeros_like(keys_g))

    def channels_of(head):
        return pl.ds(pl.multiple_of(head * HEAD, HEAD), HEAD)

    def fold(array, reduction):
        return reduction(array.reshape(array.shape[0] // 8, 8, array.shape[1]), axis=0)

    def stage(scoring, exping, mixing, scores_to, scores_from, exponent_to, exponent_from, row_max, total):
        inverse = 1.0 / total
        new_max = jnp.full((8, PATCH), -jnp.inf, f32)
        new_total = jnp.zeros((8, PATCH), f32)
        attended = jnp.zeros((HEAD, PATCH), f32)
        for start in range(0, PATCH, CHUNK):
            part = slice(start, start + CHUNK)
            if scoring is not None:
                group = pl.ds(pl.multiple_of(scoring // 8 * 128, 128), 128)
                scores = dot(keys_s[scoring, part, :], queries_s[group, :])
                scores_to[part, :] = scores
                new_max = jnp.maximum(new_max, fold(scores, jnp.max))
            if exping is not None:
                exponent = jnp.exp2((scores_from[part, :] - row_max) * EXP_SCALE)
                exponent_to[part, :] = exponent
                new_total = new_total + fold(exponent, jnp.sum)
            if mixing is not None:
                weights = (exponent_from[part, :] * inverse).astype(bf16)
                attended = attended + dot(values_s[channels_of(mixing), part], weights)
        if mixing is not None:
            attended_s[channels_of(mixing), :] = attended.astype(bf16)
        return jnp.max(new_max, axis=0, keepdims=True), jnp.sum(new_total, axis=0, keepdims=True)

    def two_stages(step, carry):
        head = 2 * step
        carry = stage(head + 2, head + 1, head, scores_a, scores_b, exponent_b, exponent_a, *carry)
        return stage(head + 3, head + 2, head + 1, scores_b, scores_a, exponent_a, exponent_b, *carry)

    one = jnp.ones((1, PATCH), f32)
    row_max, _ = stage(0, None, None, scores_a, None, None, None, one, one)
    carry = stage(1, 0, None, scores_b, scores_a, exponent_a, None, row_max, one)
    carry = lax.fori_loop(0, HEADS // 2 - 1, two_stages, carry)
    carry = stage(None, HEADS - 1, HEADS - 2, None, scores_b, exponent_b, exponent_a, *carry)
    stage(None, None, HEADS - 1, None, None, None, exponent_b, one, carry[1])
    attended = attended_s[...].astype(f32).T.astype(bf16)
    mixture = dot(attended[:, :HALF], proj_own_ref[...]) + dot(attended[:, HALF:], proj_other_ref[...])
    updated = (ordered + mixture).astype(bf16)
    kept_ref[...] = jnp.where(first, updated[:, :HALF], updated[:, HALF:])
    sent_ref[...] = jnp.where(first, updated[:, HALF:], updated[:, :HALF])


def call(kernel, name, outs, *args, scalars=0, scalar_outs=0, blocks={}, scratch=(), flops=10**9, vmem_bytes=VMEM_BYTES):
    vmem = pl.BlockSpec(memory_space=pltpu.VMEM)
    smem = pl.BlockSpec(memory_space=pltpu.SMEM)
    specs = [smem] * scalars + [vmem] * (len(args) - scalars)
    for number, (dims, index) in blocks.items():
        specs[number] = pl.BlockSpec(dims, functools.partial(lambda place, step: place, index), memory_space=pltpu.VMEM)
    many = isinstance(outs, list)
    return pl.pallas_call(
        kernel,
        grid=(1,),
        out_shape=outs,
        in_specs=specs,
        out_specs=[vmem] * (len(outs) - scalar_outs) + [smem] * scalar_outs if many else vmem,
        scratch_shapes=list(scratch),
        compiler_params=pltpu.CompilerParams(vmem_limit_bytes=vmem_bytes),
        cost_estimate=pl.CostEstimate(flops=flops, bytes_accessed=2 * 2**20, transcendentals=0),
        name=name,
    )(*args)


def shape(*dims, dtype=bf16):
    return jax.ShapeDtypeStruct(dims, dtype)


def exchange(message):
    width = message.shape[1]
    blocks = message.reshape(PEERS, ROWS // PEERS, width)
    return lax.all_to_all(blocks, "pts", split_axis=0, concat_axis=0, tiled=True).reshape(ROWS, width)


def swap(array):
    return lax.ppermute(array, "grp", [(0, 1), (1, 0)])


SLOTS = ((ROWS, 384), (0, 0))
LABELS = ((ROWS, 128), (0, 3))
PART = shape(PATCH, HALF)


def attend(number, core, own, other, gain, bias, qkv_own, qkv_other, proj_own, proj_other):
    qkv_block = ((None, 3, FULL, HALF), (number, 0, 0, 0))
    proj_block = ((None, HALF, FULL), (number, 0, 0))
    kept, sent = call(
        functools.partial(attention_kernel, block=number), "attention", [PART, PART],
        core, own, other, gain, bias, qkv_own, qkv_other, proj_own, proj_other,
        scalars=1, blocks={5: qkv_block, 6: qkv_block, 7: proj_block, 8: proj_block},
        scratch=[pltpu.VMEM((HEADS, PATCH, 128), bf16)] + [pltpu.VMEM((FULL, PATCH), bf16)] * 3
        + [pltpu.VMEM((PATCH, PATCH), f32)] * 4, flops=2 * 10**10,
    )
    return kept, swap(sent)


def send_back(order, core, kept, received, codes):
    kernel = functools.partial(return_kernel, order=order)
    return exchange(call(kernel, "return", shape(ROWS, 384), core, kept, received, codes, scalars=1))


def local(features, hilbert_rank, trans_rank, ln_gain, ln_bias, w_qkv, w_proj):
    core = lax.axis_index("grp").astype(jnp.int32)
    mine, theirs = (core * PATCH).reshape(1), ((1 - core) * PATCH).reshape(1)
    core = core.reshape(1)
    qkv = w_qkv.transpose(0, 2, 1, 3)
    weights = (ln_gain, ln_bias, qkv, swap(qkv), w_proj, swap(w_proj))
    message, index = call(
        send_kernel, "send", [shape(ROWS, 512), shape(8, ROWS, dtype=jnp.int32)],
        hilbert_rank.reshape(1, ROWS), trans_rank.reshape(1, ROWS), features, vmem_bytes=MOST_VMEM,
    )
    arrived = exchange(message)
    ranks, integer = shape(PATCH, 128, dtype=f32), jnp.int32
    leaving, other_ranks, code_rows, codes, parts = call(
        decode_place_kernel, "place_other",
        [PART, ranks, shape(8, ROWS, dtype=integer), shape(ROWS, 128, dtype=integer), shape(ROWS, 256)],
        theirs, arrived, arrived, scalars=1, blocks={1: SLOTS, 2: LABELS},
    )
    other = swap(leaving)
    own, own_ranks = call(
        place_kernel, "place_own", [PART, ranks], mine, arrived, code_rows, parts, scalars=1, blocks={1: SLOTS}
    )
    kept, received = attend(0, core, own, other, *weights)
    leave, most = call(
        leave_kernel, "leave", [shape(8, ROWS, dtype=integer), shape(1, 128, dtype=f32)], core, own_ranks, other_ranks,
        scalars=1,
    )
    message = exchange(
        call(direct_kernel, "direct", shape(ROWS, 768), core, kept, received, leave, most, scalars=1)
    )
    arrive = call(arrive_kernel, "arrive", shape(ROWS, 128, dtype=integer), code_rows, parts)
    leaving, full = call(
        place_direct_kernel, "direct_other", [PART, shape(1, 1, dtype=integer)], theirs, arrive, message, scalars=1,
        scalar_outs=1,
    )
    other = swap(leaving)
    own = call(place_direct_kernel, "direct_own", PART, mine, arrive, message, scalars=1)

    def by_home(own, other):
        landed = send_back(0, core, kept, received, codes)
        message = exchange(call(middle_kernel, "middle", shape(ROWS, 384), index, landed))
        other = swap(call(place_second_kernel, "second_other", PART, theirs, message, code_rows, scalars=1))
        return call(place_second_kernel, "second_own", PART, mine, message, code_rows, scalars=1), other

    own, other = lax.cond(full[0, 0] > 0, by_home, lambda own, other: (own, other), own, other)
    kept, received = attend(1, core, own, other, *weights)
    landed = send_back(1, core, kept, received, codes)
    return call(home_kernel, "home", shape(ROWS, HALF), index, landed)


def solution(mesh):
    in_specs = (
        P("pts", "grp"),
        P("pts"),
        P("pts"),
        P(),
        P(),
        P(None, None, None, "grp"),
        P(None, "grp", None),
    )
    return jax.shard_map(local, mesh=mesh, in_specs=in_specs, out_specs=P("pts", "grp"), check_vma=False)
```

```python
import functools
import math

import jax
import jax.numpy as jnp
from jax import lax
from jax.experimental import pallas as pl
from jax.experimental.pallas import tpu as pltpu
from jax.sharding import PartitionSpec as P

ROWS = 1024
PEERS = 128
HALF = 256
FULL = 512
PATCH = 512
HEADS = 32
HEAD = 16
EPSILON = 1e-05
EXP_SCALE = HEAD ** (-0.5) * math.log2(math.e)
CHUNK = 128
VMEM_BYTES = 24 * 2**20
MOST_VMEM = 60 * 2**20

DIRECT = 24


f32 = jnp.float32
bf16 = jnp.bfloat16


def iota(shape, axis):
    return lax.broadcasted_iota(jnp.int32, shape, axis)


def dot(left, right):
    return jnp.dot(left, right, preferred_element_type=f32)


def onehot(mask):
    return jnp.where(mask, 1.0, 0.0).astype(bf16)


def integers(array):
    return array.astype(jnp.int32)


def earlier_peers(owner, earlier):
    owners = onehot(iota((PEERS, ROWS), 0) == owner)
    running = dot(owners, earlier)
    return owners, integers(jnp.sum(running * owners.astype(f32), axis=0, keepdims=True))


def before():
    return onehot(iota((ROWS, ROWS), 0) < iota((ROWS, ROWS), 1))


def pack(low_mask, high_mask, rows, out_ref, to=slice(None)):
    out_ref[to, :HALF] = dot(onehot(low_mask), rows).astype(bf16)
    high = dot(onehot(high_mask), rows)
    first = (iota((high.shape[0], 128), 0) & 4) == 0
    out_ref[to, HALF:384] = jnp.where(first, high[:, :128], high[:, 128:]).astype(bf16)


def tails(message):
    tail = message[:, HALF:384].astype(f32)
    return jnp.concatenate([tail.astype(bf16), pltpu.roll(tail, ROWS - 4, 0).astype(bf16)], axis=1)


def in_chunks(body, chunk=128):
    def step(number, carry):
        body(pl.multiple_of(number * chunk, chunk))
        return carry

    lax.fori_loop(0, ROWS // chunk, step, 0)


def transposed(rows):
    rows = rows.astype(f32)
    return jnp.concatenate([rows, jnp.zeros((128 - rows.shape[0], ROWS), f32)], axis=0).T


def send_kernel(hilbert_ref, trans_ref, features_ref, message_ref, index_ref):
    features = features_ref[...]
    earlier = before()
    ranks = [hilbert_ref[...], trans_ref[...]]
    owners = [lax.shift_right_logical(rank, 10) for rank in ranks]
    highs = [lax.shift_right_logical(rank, 5) & 31 for rank in ranks]
    lows = [rank & 31 for rank in ranks]
    values = [[highs[0] + 1, lows[0], owners[1], highs[1], lows[1]], [highs[1] + 1, lows[1], owners[0]]]
    steps = iota((16, ROWS), 0)
    labels = jnp.zeros((PEERS, 128), f32)
    index = []
    for order in range(2):
        peers, slot = earlier_peers(owners[order], earlier)
        index.append(jnp.where(slot < 8, owners[order] * 8 + slot, -1))
        index.append(jnp.where((slot >= 8) & (slot < 12), owners[order] * 8 + slot - 8, -1))
        here = steps == slot
        spread = jnp.concatenate(
            [jnp.where(here, value, 0).astype(f32).astype(bf16) for value in values[order]], axis=0
        )
        empty = [jnp.zeros((16 * (8 - len(values[order])), ROWS), bf16)]
        spread = jnp.concatenate([spread] + empty if order == 0 else empty + [spread], axis=0)
        labels += lax.dot_general(peers, spread, (((1,), (1,)), ((), ())), preferred_element_type=f32)
    index_ref[...] = jnp.concatenate(index + [jnp.full((4, ROWS), -1, jnp.int32)], axis=0)
    rows = iota((ROWS, ROWS), 0)
    pack(rows == index[0], (rows & ~4) == index[1], features, message_ref)
    labels = jnp.broadcast_to(labels[:, None, :], (PEERS, 8, 128)).reshape(ROWS, 128)
    message_ref[:, 384:] = labels.astype(bf16)


def decode(labels):
    labels = labels.astype(f32)
    row, lane = iota((ROWS, 128), 0), iota((ROWS, 128), 1)
    low = jnp.where((lane & 15) == (row & 7), labels, 0.0).astype(bf16)
    high = jnp.where((lane & 15) == 8 + (row & 3), labels, 0.0).astype(bf16)
    value, column = lax.shift_right_logical(iota((128, 128), 0), 4), iota((128, 128), 1)

    def table(entries):
        weights = jnp.zeros((128, 128), f32)
        for to, source, weight in entries:
            weights += jnp.where((column == to) & (value == source), float(weight), 0.0)
        return weights.astype(bf16)

    entries = [(0, 0, 32), (0, 1, 1), (2, 2, 1024), (2, 3, 32), (2, 4, 1), (4, 5, 32), (4, 6, 1), (6, 7, 1)]
    codes = dot(low, table(entries)) + dot(high, table([(to + 1, v, w) for to, v, w in entries]))
    codes = integers(codes.T[:8])
    kind = iota((8, ROWS), 0)
    return codes - jnp.where((kind < 2) | (kind == 4) | (kind == 5), 32, 0)


def position_masks(codes, order, targets):
    low, high = codes[4 * order:4 * order + 1], codes[4 * order + 1:4 * order + 2]
    return targets == low, targets == jnp.where((iota((1, ROWS), 1) & 4) == 0, high, -1)


def place_rows(base_ref, message_ref, codes, out_ref, ranks_ref):
    def parts(rank):
        device = lax.shift_right_logical(rank, 10)
        return transposed(jnp.concatenate([device, lax.shift_right_logical(rank, 5) & 31, rank & 31], axis=0))

    message = message_ref[...]
    low_mask, high_mask = position_masks(codes, 0, iota((PATCH, ROWS), 0) + base_ref[0])
    low = jnp.concatenate([message[:, :HALF], parts(codes[2:3]).astype(bf16)], axis=1)
    high = jnp.concatenate([tails(message), parts(codes[3:4]).astype(bf16)], axis=1)
    placed = dot(onehot(low_mask), low) + dot(onehot(high_mask), high)
    out_ref[...] = placed[:, :HALF].astype(bf16)
    ranks_ref[...] = placed[:, HALF:].T[:8]


def decode_place_kernel(base_ref, message_ref, labels_ref, out_ref, ranks_ref, codes_ref):
    codes = decode(labels_ref[...])
    codes_ref[...] = codes
    place_rows(base_ref, message_ref, codes, out_ref, ranks_ref)


def place_kernel(base_ref, message_ref, codes_ref, out_ref, ranks_ref):
    place_rows(base_ref, message_ref, codes_ref[...], out_ref, ranks_ref)


def in_order(core_ref, own, other, axis=0):
    first = core_ref[0] == 0
    return jnp.concatenate([jnp.where(first, own, other), jnp.where(first, other, own)], axis=axis)


def return_kernel(core_ref, kept_ref, received_ref, codes_ref, out_ref):
    rows = in_order(core_ref, kept_ref[...], received_ref[...])
    codes = integers(transposed(codes_ref[4:6, :]))
    targets = iota((ROWS, ROWS), 1)
    pack(targets == codes[:, 0:1], targets == codes[:, 1:2], rows, out_ref)


def home_kernel(index_ref, message_ref, out_ref):
    message = message_ref[...]
    columns = integers(transposed(index_ref[2:4, :]))
    sources = iota((ROWS, ROWS), 1)
    placed = dot(onehot(sources == columns[:, 0:1]), message[:, :HALF])
    placed += dot(onehot(sources == columns[:, 1:2]), tails(message))
    out_ref[...] = placed.astype(bf16)


def slow_return_kernel(core_ref, kept_ref, received_ref, codes_ref, out_ref, columns_s):
    rows = in_order(core_ref, kept_ref[...], received_ref[...])
    columns_s[...] = integers(transposed(codes_ref[0:2, :]))

    def some(start):
        columns = columns_s[pl.ds(start, 128), :]
        targets = iota((128, ROWS), 1)
        pack(targets == columns[:, 0:1], targets == columns[:, 1:2], rows, out_ref, pl.ds(start, 128))

    in_chunks(some)


def slow_middle_kernel(index_ref, message_ref, out_ref, columns_s, rows_s):
    message = message_ref[...]
    tail = tails(message)
    columns_s[...] = integers(transposed(index_ref[0:2, :]))
    low, high = index_ref[2:3, :], index_ref[3:4, :]

    def home(start):
        columns = columns_s[pl.ds(start, 128), :]
        sources = iota((128, ROWS), 1)
        placed = dot(onehot(sources == columns[:, 0:1]), message[:, :HALF])
        rows_s[pl.ds(start, 128), :] = (placed + dot(onehot(sources == columns[:, 1:2]), tail)).astype(bf16)

    def leave(start):
        targets = iota((128, ROWS), 0) + start
        pack(targets == low, (targets & ~4) == high, rows_s[...], out_ref, pl.ds(start, 128))

    in_chunks(home)
    in_chunks(leave)


def slow_place_kernel(message_ref, codes_ref, out_ref):
    message, codes = message_ref[...], codes_ref[...]
    tail = tails(message)

    def some(start):
        low, high = position_masks(codes, 1, iota((128, ROWS), 0) + start)
        placed = dot(onehot(low), message[:, :HALF]) + dot(onehot(high), tail)
        out_ref[pl.ds(start, 128), :] = placed.astype(bf16)

    in_chunks(some)


def direct_index(owner, slot):
    row, third = owner * 8 + (slot & 7), lax.shift_right_logical(slot, 3)
    return jnp.where(iota((8, ROWS), 0) == third, row, -1)


def leave_kernel(core_ref, own_ref, other_ref, index_ref, most_ref, ranks_s):
    parts = integers(in_order(core_ref, own_ref[...], other_ref[...], axis=1))
    owner = parts[0:1]
    rank = owner * 1024 + parts[1:2] * 32 + parts[2:3]
    ranks_s[...] = integers(transposed(rank))
    ahead = jnp.zeros((8, ROWS), f32)
    for start in range(0, ROWS, 512):
        column = ranks_s[start:start + 512, 0:1]
        here = jnp.where((column >= owner * 1024) & (column < rank), 1.0, 0.0)
        ahead = ahead + jnp.sum(here.reshape(64, 8, ROWS), axis=0)
    slot = integers(jnp.sum(ahead, axis=0, keepdims=True))
    index_ref[...] = direct_index(owner, slot)
    most_ref[...] = jnp.broadcast_to(jnp.max(slot.astype(f32), axis=1, keepdims=True) + 1.0, (1, 128))


def direct_kernel(core_ref, kept_ref, received_ref, index_ref, most_ref, out_ref):
    rows = in_order(core_ref, kept_ref[...], received_ref[...])
    targets = iota((ROWS, ROWS), 0)
    for third in range(DIRECT // 8):
        columns = slice(third * HALF, (third + 1) * HALF)
        packed = dot(onehot(targets == index_ref[third:third + 1]), rows)
        if third == 0:
            packed = jnp.where(most_ref[:, :1] > DIRECT, jnp.inf, packed)
        out_ref[:, columns] = packed.astype(bf16)


def arrive_kernel(codes_ref, index_ref, owners_s):
    codes = codes_ref[...]
    low_owner = transposed(codes[6:7]).astype(bf16)
    high_owner = transposed(codes[7:8]).astype(bf16)

    def some(start):
        low, high = position_masks(codes, 1, iota((128, ROWS), 0) + start)
        owners_s[pl.ds(start, 128), :] = dot(onehot(low), low_owner) + dot(onehot(high), high_owner)

    in_chunks(some)
    owner = integers(owners_s[...].T[0:1])
    _, slot = earlier_peers(owner, before())
    index_ref[...] = direct_index(owner, slot)


def place_direct_kernel(base_ref, index_ref, message_ref, out_ref, *full_ref):
    if full_ref:
        largest = jnp.max(jnp.abs(message_ref[:, :128].astype(f32)))
        full_ref[0][0, 0] = jnp.where(largest == jnp.inf, 1, 0)
    index = integers(transposed(index_ref[0:3, :]))
    index = jnp.where(base_ref[0] == 0, index[:PATCH], index[PATCH:])
    sources = iota((PATCH, ROWS), 1)
    placed = jnp.zeros((PATCH, HALF), f32)
    for third in range(DIRECT // 8):
        mask = sources == index[:, third:third + 1]
        placed += dot(onehot(mask), message_ref[:, third * HALF:(third + 1) * HALF])
    out_ref[...] = placed.astype(bf16)


def attention_kernel(
    core_ref, own_ref, other_ref, gain_ref, bias_ref, qkv_own_ref, qkv_other_ref, proj_own_ref, proj_other_ref,
    kept_ref, sent_ref, keys_s, queries_s, values_s, attended_s, scores_a, scores_b, exponent_a, exponent_b, *, block,
):
    first = core_ref[0] == 0
    own, other = own_ref[...], other_ref[...]
    ordered = jnp.concatenate([jnp.where(first, own, other), jnp.where(first, other, own)], axis=1)
    ordered = ordered.astype(f32)
    average = jnp.sum(ordered, axis=1, keepdims=True) / FULL
    variance = jnp.sum(ordered * ordered, axis=1, keepdims=True) / FULL - average * average
    normed = (ordered - average) * lax.rsqrt(variance + EPSILON) * gain_ref[block:block + 1] + bias_ref[block:block + 1]
    normed = normed.astype(bf16)
    lane = iota((PATCH, 128), 1)
    for part, weight_ref in enumerate((qkv_own_ref, qkv_other_ref)):
        channels = slice(part * HALF, (part + 1) * HALF)
        queries_s[channels, :] = dot(normed, weight_ref[0]).T.astype(bf16)
        values_s[channels, :] = dot(normed, weight_ref[2]).T.astype(bf16)
        keys = dot(normed, weight_ref[1]).astype(bf16)
        for group in range(2):
            keys_g = keys[:, group * 128:(group + 1) * 128]
            for head in range(8):
                keys_s[part * 16 + group * 8 + head] = jnp.where(lane >> 4 == head, keys_g, jnp.zeros_like(keys_g))

    def channels_of(head):
        return pl.ds(pl.multiple_of(head * HEAD, HEAD), HEAD)

    def fold(array, reduction):
        return reduction(array.reshape(array.shape[0] // 8, 8, array.shape[1]), axis=0)

    def stage(scoring, exping, mixing, scores_to, scores_from, exponent_to, exponent_from, row_max, total):
        inverse = 1.0 / total
        new_max = jnp.full((8, PATCH), -jnp.inf, f32)
        new_total = jnp.zeros((8, PATCH), f32)
        attended = jnp.zeros((HEAD, PATCH), f32)
        for start in range(0, PATCH, CHUNK):
            part = slice(start, start + CHUNK)
            if scoring is not None:
                group = pl.ds(pl.multiple_of((scoring >> 3) * 128, 128), 128)
                scores = dot(keys_s[scoring, part, :], queries_s[group, :])
                scores_to[part, :] = scores
                new_max = jnp.maximum(new_max, fold(scores, jnp.max))
            if exping is not None:
                exponent = jnp.exp2((scores_from[part, :] - row_max) * EXP_SCALE)
                exponent_to[part, :] = exponent
                new_total = new_total + fold(exponent, jnp.sum)
            if mixing is not None:
                weights = (exponent_from[part, :] * inverse).astype(bf16)
                attended = attended + dot(values_s[channels_of(mixing), part], weights)
        if mixing is not None:
            attended_s[channels_of(mixing), :] = attended.astype(bf16)
        return jnp.max(new_max, axis=0, keepdims=True), jnp.sum(new_total, axis=0, keepdims=True)

    def two_stages(step, carry):
        head = 2 * step
        carry = stage(head + 2, head + 1, head, scores_a, scores_b, exponent_b, exponent_a, *carry)
        return stage(head + 3, head + 2, head + 1, scores_b, scores_a, exponent_a, exponent_b, *carry)

    one = jnp.ones((1, PATCH), f32)
    row_max, _ = stage(0, None, None, scores_a, None, None, None, one, one)
    carry = stage(1, 0, None, scores_b, scores_a, exponent_a, None, row_max, one)
    carry = lax.fori_loop(0, HEADS // 2 - 1, two_stages, carry)
    carry = stage(None, HEADS - 1, HEADS - 2, None, scores_b, exponent_b, exponent_a, *carry)
    stage(None, None, HEADS - 1, None, None, None, exponent_b, one, carry[1])
    attended = attended_s[...].astype(f32).T.astype(bf16)
    mixture = dot(attended[:, :HALF], proj_own_ref[...]) + dot(attended[:, HALF:], proj_other_ref[...])
    updated = (ordered + mixture).astype(bf16)
    kept_ref[...] = jnp.where(first, updated[:, :HALF], updated[:, HALF:])
    sent_ref[...] = jnp.where(first, updated[:, HALF:], updated[:, :HALF])


def call(kernel, name, outs, *args, scalars=0, scalar_outs=0, blocks={}, scratch=(), flops=10**9, vmem_bytes=VMEM_BYTES):
    vmem = pl.BlockSpec(memory_space=pltpu.VMEM)
    smem = pl.BlockSpec(memory_space=pltpu.SMEM)
    specs = [smem] * scalars + [vmem] * (len(args) - scalars)
    for number, (dims, index) in blocks.items():
        specs[number] = pl.BlockSpec(dims, functools.partial(lambda place, step: place, index), memory_space=pltpu.VMEM)
    many = isinstance(outs, list)
    return pl.pallas_call(
        kernel,
        grid=(1,),
        out_shape=outs,
        in_specs=specs,
        out_specs=[vmem] * (len(outs) - scalar_outs) + [smem] * scalar_outs if many else vmem,
        scratch_shapes=list(scratch),
        compiler_params=pltpu.CompilerParams(vmem_limit_bytes=vmem_bytes),
        cost_estimate=pl.CostEstimate(flops=flops, bytes_accessed=2 * 2**20, transcendentals=0),
        name=name,
    )(*args)


def shape(*dims, dtype=bf16):
    return jax.ShapeDtypeStruct(dims, dtype)


def exchange(message):
    width = message.shape[1]
    blocks = message.reshape(PEERS, ROWS // PEERS, width)
    return lax.all_to_all(blocks, "pts", split_axis=0, concat_axis=0, tiled=True).reshape(ROWS, width)


def swap(array):
    return lax.ppermute(array, "grp", [(0, 1), (1, 0)])


SLOTS = ((ROWS, 384), (0, 0))
LABELS = ((ROWS, 128), (0, 3))
PART = shape(PATCH, HALF)


def attend(number, core, own, other, gain, bias, qkv_own, qkv_other, proj_own, proj_other):
    qkv_block = ((None, 3, FULL, HALF), (number, 0, 0, 0))
    proj_block = ((None, HALF, FULL), (number, 0, 0))
    kept, sent = call(
        functools.partial(attention_kernel, block=number), "attention", [PART, PART],
        core, own, other, gain, bias, qkv_own, qkv_other, proj_own, proj_other,
        scalars=1, blocks={5: qkv_block, 6: qkv_block, 7: proj_block, 8: proj_block},
        scratch=[pltpu.VMEM((HEADS, PATCH, 128), bf16)] + [pltpu.VMEM((FULL, PATCH), bf16)] * 3
        + [pltpu.VMEM((PATCH, PATCH), f32)] * 4, flops=2 * 10**10,
    )
    return kept, swap(sent)


def local(features, hilbert_rank, trans_rank, ln_gain, ln_bias, w_qkv, w_proj):
    core = lax.axis_index("grp").astype(jnp.int32)
    mine, theirs = (core * PATCH).reshape(1), ((1 - core) * PATCH).reshape(1)
    core = core.reshape(1)
    qkv = w_qkv.transpose(0, 2, 1, 3)
    weights = (ln_gain, ln_bias, qkv, swap(qkv), w_proj, swap(w_proj))
    message, index = call(
        send_kernel, "send", [shape(ROWS, 512), shape(8, ROWS, dtype=jnp.int32)],
        hilbert_rank.reshape(1, ROWS), trans_rank.reshape(1, ROWS), features, vmem_bytes=MOST_VMEM,
    )
    arrived = exchange(message)
    ranks, table = shape(8, PATCH, dtype=f32), shape(8, ROWS, dtype=jnp.int32)
    columns = pltpu.VMEM((ROWS, 128), jnp.int32)
    leaving, other_ranks, codes = call(
        decode_place_kernel, "place_other", [PART, ranks, table], theirs, arrived, arrived, scalars=1,
        blocks={1: SLOTS, 2: LABELS},
    )
    other = swap(leaving)
    own, own_ranks = call(
        place_kernel, "place_own", [PART, ranks], mine, arrived, codes, scalars=1, blocks={1: SLOTS}
    )
    kept, received = attend(0, core, own, other, *weights)
    leave, most = call(
        leave_kernel, "leave", [table, shape(1, 128, dtype=f32)], core, own_ranks, other_ranks, scalars=1,
        scratch=[columns],
    )
    message = exchange(
        call(direct_kernel, "direct", shape(ROWS, 768), core, kept, received, leave, most, scalars=1)
    )
    arrive = call(arrive_kernel, "arrive", table, codes, scratch=[pltpu.VMEM((ROWS, 128), f32)])
    leaving, full = call(
        place_direct_kernel, "direct_other", [PART, shape(1, 1, dtype=jnp.int32)], theirs, arrive, message, scalars=1,
        scalar_outs=1,
    )
    other = swap(leaving)
    own = call(place_direct_kernel, "direct_own", PART, mine, arrive, message, scalars=1)

    def by_home(own, other):
        message = exchange(call(
            slow_return_kernel, "slow_return", shape(ROWS, 384), core, kept, received, codes, scalars=1,
            scratch=[columns],
        ))
        message = exchange(call(
            slow_middle_kernel, "slow_middle", shape(ROWS, 384), index, message,
            scratch=[columns, pltpu.VMEM((ROWS, HALF), bf16)],
        ))
        rows = call(slow_place_kernel, "slow_place", shape(ROWS, HALF), message, codes)
        leaving = lax.dynamic_slice_in_dim(rows, theirs[0], PATCH)
        return lax.dynamic_slice_in_dim(rows, mine[0], PATCH), swap(leaving)

    own, other = lax.cond(full[0, 0] > 0, by_home, lambda own, other: (own, other), own, other)
    kept, received = attend(1, core, own, other, *weights)
    landed = exchange(call(return_kernel, "return", shape(ROWS, 384), core, kept, received, codes, scalars=1))
    return call(home_kernel, "home", shape(ROWS, HALF), index, landed)


def solution(mesh):
    in_specs = (
        P("pts", "grp"),
        P("pts"),
        P("pts"),
        P(),
        P(),
        P(None, None, None, "grp"),
        P(None, "grp", None),
    )
    return jax.shard_map(local, mesh=mesh, in_specs=in_specs, out_specs=P("pts", "grp"), check_vma=False)
```

```python
import functools
import math

import jax
import jax.numpy as jnp
from jax import lax
from jax.experimental import pallas as pl
from jax.experimental.pallas import tpu as pltpu
from jax.sharding import PartitionSpec as P

ROWS = 1024
PEERS = 128
HALF = 256
FULL = 512
PATCH = 512
HEADS = 32
HEAD = 16
EPSILON = 1e-05
EXP_SCALE = HEAD ** (-0.5) * math.log2(math.e)
CHUNK = 128
SLOW = 32
VMEM_BYTES = 24 * 2**20
MOST_VMEM = 60 * 2**20

DIRECT = 24


f32 = jnp.float32
bf16 = jnp.bfloat16


def iota(shape, axis):
    return lax.broadcasted_iota(jnp.int32, shape, axis)


def dot(left, right):
    return jnp.dot(left, right, preferred_element_type=f32)


def onehot(mask):
    return jnp.where(mask, 1.0, 0.0).astype(bf16)


def integers(array):
    return array.astype(jnp.int32)


def earlier_peers(owner, earlier):
    owners = onehot(iota((PEERS, ROWS), 0) == owner)
    running = dot(owners, earlier)
    return owners, integers(jnp.sum(running * owners.astype(f32), axis=0, keepdims=True))


def before():
    return onehot(iota((ROWS, ROWS), 0) < iota((ROWS, ROWS), 1))


def pack(low_mask, high_mask, rows, out_ref, to=slice(None)):
    out_ref[to, :HALF] = dot(onehot(low_mask), rows).astype(bf16)
    high = dot(onehot(high_mask), rows)
    first = (iota((high.shape[0], 128), 0) & 4) == 0
    out_ref[to, HALF:384] = jnp.where(first, high[:, :128], high[:, 128:]).astype(bf16)


def tails(message):
    tail = message[:, HALF:384].astype(f32)
    return jnp.concatenate([tail.astype(bf16), pltpu.roll(tail, ROWS - 4, 0).astype(bf16)], axis=1)


def in_chunks(body, chunk):
    def step(number, carry):
        body(pl.multiple_of(number * chunk, chunk))
        return carry

    lax.fori_loop(0, ROWS // chunk, step, 0)


def transposed(rows):
    rows = rows.astype(f32)
    return jnp.concatenate([rows, jnp.zeros((128 - rows.shape[0], ROWS), f32)], axis=0).T


def send_kernel(hilbert_ref, trans_ref, features_ref, message_ref, index_ref):
    features = features_ref[...]
    earlier = before()
    ranks = [hilbert_ref[...], trans_ref[...]]
    owners = [lax.shift_right_logical(rank, 10) for rank in ranks]
    highs = [lax.shift_right_logical(rank, 5) & 31 for rank in ranks]
    lows = [rank & 31 for rank in ranks]
    values = [[highs[0] + 1, lows[0], owners[1], highs[1], lows[1]], [highs[1] + 1, lows[1], owners[0]]]
    steps = iota((16, ROWS), 0)
    labels = jnp.zeros((PEERS, 128), f32)
    index = []
    for order in range(2):
        peers, slot = earlier_peers(owners[order], earlier)
        index.append(jnp.where(slot < 8, owners[order] * 8 + slot, -1))
        index.append(jnp.where((slot >= 8) & (slot < 12), owners[order] * 8 + slot - 8, -1))
        here = steps == slot
        spread = jnp.concatenate(
            [jnp.where(here, value, 0).astype(f32).astype(bf16) for value in values[order]], axis=0
        )
        empty = [jnp.zeros((16 * (8 - len(values[order])), ROWS), bf16)]
        spread = jnp.concatenate([spread] + empty if order == 0 else empty + [spread], axis=0)
        labels += lax.dot_general(peers, spread, (((1,), (1,)), ((), ())), preferred_element_type=f32)
    index_ref[...] = jnp.concatenate(index + [jnp.full((4, ROWS), -1, jnp.int32)], axis=0)
    rows = iota((ROWS, ROWS), 0)
    pack(rows == index[0], (rows & ~4) == index[1], features, message_ref)
    labels = jnp.broadcast_to(labels[:, None, :], (PEERS, 8, 128)).reshape(ROWS, 128)
    message_ref[:, 384:] = labels.astype(bf16)


def decode(labels):
    labels = labels.astype(f32)
    row, lane = iota((ROWS, 128), 0), iota((ROWS, 128), 1)
    low = jnp.where((lane & 15) == (row & 7), labels, 0.0).astype(bf16)
    high = jnp.where((lane & 15) == 8 + (row & 3), labels, 0.0).astype(bf16)
    value, column = lax.shift_right_logical(iota((128, 128), 0), 4), iota((128, 128), 1)

    def table(entries):
        weights = jnp.zeros((128, 128), f32)
        for to, source, weight in entries:
            weights += jnp.where((column == to) & (value == source), float(weight), 0.0)
        return weights.astype(bf16)

    entries = [(0, 0, 32), (0, 1, 1), (2, 2, 1024), (2, 3, 32), (2, 4, 1), (4, 5, 32), (4, 6, 1), (6, 7, 1)]
    codes = dot(low, table(entries)) + dot(high, table([(to + 1, v, w) for to, v, w in entries]))
    codes = integers(codes.T[:8])
    kind = iota((8, ROWS), 0)
    return codes - jnp.where((kind < 2) | (kind == 4) | (kind == 5), 32, 0)


def position_masks(codes, order, targets):
    low, high = codes[4 * order:4 * order + 1], codes[4 * order + 1:4 * order + 2]
    return targets == low, targets == jnp.where((iota((1, ROWS), 1) & 4) == 0, high, -1)


def place_rows(base_ref, message_ref, codes, out_ref, ranks_ref):
    def parts(rank):
        device = lax.shift_right_logical(rank, 10)
        return transposed(jnp.concatenate([device, lax.shift_right_logical(rank, 5) & 31, rank & 31], axis=0))

    message = message_ref[...]
    low_mask, high_mask = position_masks(codes, 0, iota((PATCH, ROWS), 0) + base_ref[0])
    low = jnp.concatenate([message[:, :HALF], parts(codes[2:3]).astype(bf16)], axis=1)
    high = jnp.concatenate([tails(message), parts(codes[3:4]).astype(bf16)], axis=1)
    placed = dot(onehot(low_mask), low) + dot(onehot(high_mask), high)
    out_ref[...] = placed[:, :HALF].astype(bf16)
    ranks_ref[...] = placed[:, HALF:].T[:8]


def decode_place_kernel(base_ref, message_ref, labels_ref, out_ref, ranks_ref, codes_ref):
    codes = decode(labels_ref[...])
    codes_ref[...] = codes
    place_rows(base_ref, message_ref, codes, out_ref, ranks_ref)


def place_kernel(base_ref, message_ref, codes_ref, out_ref, ranks_ref):
    place_rows(base_ref, message_ref, codes_ref[...], out_ref, ranks_ref)


def in_order(core_ref, own, other, axis=0):
    first = core_ref[0] == 0
    return jnp.concatenate([jnp.where(first, own, other), jnp.where(first, other, own)], axis=axis)


def return_kernel(core_ref, kept_ref, received_ref, codes_ref, out_ref):
    rows = in_order(core_ref, kept_ref[...], received_ref[...])
    codes = integers(transposed(codes_ref[4:6, :]))
    targets = iota((ROWS, ROWS), 1)
    pack(targets == codes[:, 0:1], targets == codes[:, 1:2], rows, out_ref)


def home_kernel(index_ref, message_ref, out_ref):
    message = message_ref[...]
    columns = integers(transposed(index_ref[2:4, :]))
    sources = iota((ROWS, ROWS), 1)
    placed = dot(onehot(sources == columns[:, 0:1]), message[:, :HALF])
    placed += dot(onehot(sources == columns[:, 1:2]), tails(message))
    out_ref[...] = placed.astype(bf16)


def slow_return_kernel(core_ref, kept_ref, received_ref, codes_ref, out_ref, columns_s):
    rows = in_order(core_ref, kept_ref[...], received_ref[...])
    columns_s[...] = integers(transposed(codes_ref[0:2, :]))

    def some(start):
        columns = columns_s[pl.ds(start, SLOW), :]
        targets = iota((SLOW, ROWS), 1)
        pack(targets == columns[:, 0:1], targets == columns[:, 1:2], rows, out_ref, pl.ds(start, SLOW))

    in_chunks(some, SLOW)


def slow_middle_kernel(index_ref, message_ref, out_ref, columns_s, rows_s):
    message = message_ref[...]
    tail = tails(message)
    columns_s[...] = integers(transposed(index_ref[0:2, :]))
    low, high = index_ref[2:3, :], index_ref[3:4, :]

    def home(start):
        columns = columns_s[pl.ds(start, SLOW), :]
        sources = iota((SLOW, ROWS), 1)
        placed = dot(onehot(sources == columns[:, 0:1]), message[:, :HALF])
        rows_s[pl.ds(start, SLOW), :] = (placed + dot(onehot(sources == columns[:, 1:2]), tail)).astype(bf16)

    def leave(start):
        targets = iota((SLOW, ROWS), 0) + start
        pack(targets == low, (targets & ~4) == high, rows_s[...], out_ref, pl.ds(start, SLOW))

    in_chunks(home, SLOW)
    in_chunks(leave, SLOW)


def slow_place_kernel(message_ref, codes_ref, out_ref):
    message, codes = message_ref[...], codes_ref[...]
    tail = tails(message)

    def some(start):
        low, high = position_masks(codes, 1, iota((SLOW, ROWS), 0) + start)
        placed = dot(onehot(low), message[:, :HALF]) + dot(onehot(high), tail)
        out_ref[pl.ds(start, SLOW), :] = placed.astype(bf16)

    in_chunks(some, SLOW)


def direct_index(owner, slot):
    row, third = owner * 8 + (slot & 7), lax.shift_right_logical(slot, 3)
    return jnp.where(iota((8, ROWS), 0) == third, row, -1)


def leave_kernel(core_ref, own_ref, other_ref, index_ref, most_ref, ranks_s):
    parts = integers(in_order(core_ref, own_ref[...], other_ref[...], axis=1))
    owner = parts[0:1]
    rank = owner * 1024 + parts[1:2] * 32 + parts[2:3]
    ranks_s[...] = integers(transposed(rank))
    ahead = jnp.zeros((8, ROWS), f32)
    for start in range(0, ROWS, 512):
        column = ranks_s[start:start + 512, 0:1]
        here = jnp.where((column >= owner * 1024) & (column < rank), 1.0, 0.0)
        ahead = ahead + jnp.sum(here.reshape(64, 8, ROWS), axis=0)
    slot = integers(jnp.sum(ahead, axis=0, keepdims=True))
    index_ref[...] = direct_index(owner, slot)
    most_ref[...] = jnp.broadcast_to(jnp.max(slot.astype(f32), axis=1, keepdims=True) + 1.0, (1, 128))


def direct_kernel(core_ref, kept_ref, received_ref, index_ref, most_ref, out_ref):
    rows = in_order(core_ref, kept_ref[...], received_ref[...])
    targets = iota((ROWS, ROWS), 0)
    for third in range(DIRECT // 8):
        columns = slice(third * HALF, (third + 1) * HALF)
        packed = dot(onehot(targets == index_ref[third:third + 1]), rows)
        if third == 0:
            packed = jnp.where(most_ref[:, :1] > DIRECT, jnp.inf, packed)
        out_ref[:, columns] = packed.astype(bf16)


def arrive_kernel(codes_ref, index_ref, owners_s):
    codes = codes_ref[...]
    low_owner = transposed(codes[6:7]).astype(bf16)
    high_owner = transposed(codes[7:8]).astype(bf16)

    def some(start):
        low, high = position_masks(codes, 1, iota((64, ROWS), 0) + start)
        owners_s[pl.ds(start, 64), :] = dot(onehot(low), low_owner) + dot(onehot(high), high_owner)

    in_chunks(some, 64)
    owner = integers(owners_s[...].T[0:1])
    _, slot = earlier_peers(owner, before())
    index_ref[...] = direct_index(owner, slot)


def place_direct_kernel(base_ref, index_ref, message_ref, out_ref, *full_ref):
    if full_ref:
        largest = jnp.max(jnp.abs(message_ref[:, :128].astype(f32)))
        full_ref[0][0, 0] = jnp.where(largest == jnp.inf, 1, 0)
    index = integers(transposed(index_ref[0:3, :]))
    index = jnp.where(base_ref[0] == 0, index[:PATCH], index[PATCH:])
    sources = iota((PATCH, ROWS), 1)
    placed = jnp.zeros((PATCH, HALF), f32)
    for third in range(DIRECT // 8):
        mask = sources == index[:, third:third + 1]
        placed += dot(onehot(mask), message_ref[:, third * HALF:(third + 1) * HALF])
    out_ref[...] = placed.astype(bf16)


def attention_kernel(
    core_ref, own_ref, other_ref, gain_ref, bias_ref, qkv_own_ref, qkv_other_ref, proj_own_ref, proj_other_ref,
    kept_ref, sent_ref, keys_s, queries_s, values_s, attended_s, weights_s, scores_a, scores_b, exponent_a, exponent_b, *, block,
):
    first = core_ref[0] == 0
    own, other = own_ref[...], other_ref[...]
    ordered = jnp.concatenate([jnp.where(first, own, other), jnp.where(first, other, own)], axis=1)
    ordered = ordered.astype(f32)
    average = jnp.sum(ordered, axis=1, keepdims=True) / FULL
    variance = jnp.sum(ordered * ordered, axis=1, keepdims=True) / FULL - average * average
    normed = (ordered - average) * lax.rsqrt(variance + EPSILON) * gain_ref[block:block + 1] + bias_ref[block:block + 1]
    normed = normed.astype(bf16)
    lane = iota((PATCH, 128), 1)
    for part, weight_ref in enumerate((qkv_own_ref, qkv_other_ref)):
        channels = slice(part * HALF, (part + 1) * HALF)
        queries_s[channels, :] = dot(normed, weight_ref[0]).T.astype(bf16)
        values_s[channels, :] = dot(normed, weight_ref[2]).T.astype(bf16)
        keys = dot(normed, weight_ref[1]).astype(bf16)
        for group in range(2):
            keys_g = keys[:, group * 128:(group + 1) * 128]
            for head in range(8):
                keys_s[part * 16 + group * 8 + head] = jnp.where(lane >> 4 == head, keys_g, jnp.zeros_like(keys_g))

    def channels_of(head):
        return pl.ds(pl.multiple_of(head * HEAD, HEAD), HEAD)

    def fold(array, reduction):
        return reduction(array.reshape(array.shape[0] // 8, 8, array.shape[1]), axis=0)

    def stage(scoring, exping, mixing, scores_to, scores_from, exponent_to, exponent_from, row_max, total):
        inverse = 1.0 / total
        new_max = jnp.full((8, PATCH), -jnp.inf, f32)
        new_total = jnp.zeros((8, PATCH), f32)
        attended = jnp.zeros((HEAD, PATCH), f32)
        for start in range(0, PATCH, CHUNK):
            part = slice(start, start + CHUNK)
            if scoring is not None:
                group = pl.ds(pl.multiple_of((scoring >> 3) * 128, 128), 128)
                scores = dot(keys_s[scoring, part, :], queries_s[group, :])
                scores_to[part, :] = scores
                new_max = jnp.maximum(new_max, fold(scores, jnp.max))
            if mixing is not None:
                weights_s[part, :] = (exponent_from[part, :] * inverse).astype(bf16)
            if exping is not None:
                exponent = jnp.exp2((scores_from[part, :] - row_max) * EXP_SCALE)
                exponent_to[part, :] = exponent
                new_total = new_total + fold(exponent, jnp.sum)
            if mixing is not None and start % (2 * CHUNK) == CHUNK:
                both = slice(start - CHUNK, start + CHUNK)
                attended = attended + dot(values_s[channels_of(mixing), both], weights_s[both, :])
        if mixing is not None:
            attended_s[channels_of(mixing), :] = attended.astype(bf16)
        return jnp.max(new_max, axis=0, keepdims=True), jnp.sum(new_total, axis=0, keepdims=True)

    def two_stages(step, carry):
        head = 2 * step
        carry = stage(head + 2, head + 1, head, scores_a, scores_b, exponent_b, exponent_a, *carry)
        return stage(head + 3, head + 2, head + 1, scores_b, scores_a, exponent_a, exponent_b, *carry)

    one = jnp.ones((1, PATCH), f32)
    row_max, _ = stage(0, None, None, scores_a, None, None, None, one, one)
    carry = stage(1, 0, None, scores_b, scores_a, exponent_a, None, row_max, one)
    carry = lax.fori_loop(0, HEADS // 2 - 1, two_stages, carry)
    carry = stage(None, HEADS - 1, HEADS - 2, None, scores_b, exponent_b, exponent_a, *carry)
    stage(None, None, HEADS - 1, None, None, None, exponent_b, one, carry[1])
    attended = attended_s[...].astype(f32).T.astype(bf16)
    mixture = dot(attended[:, :HALF], proj_own_ref[...]) + dot(attended[:, HALF:], proj_other_ref[...])
    updated = (ordered + mixture).astype(bf16)
    kept_ref[...] = jnp.where(first, updated[:, :HALF], updated[:, HALF:])
    sent_ref[...] = jnp.where(first, updated[:, HALF:], updated[:, :HALF])


def call(kernel, name, outs, *args, scalars=0, scalar_outs=0, blocks={}, scratch=(), flops=10**9, vmem_bytes=VMEM_BYTES):
    vmem = pl.BlockSpec(memory_space=pltpu.VMEM)
    smem = pl.BlockSpec(memory_space=pltpu.SMEM)
    specs = [smem] * scalars + [vmem] * (len(args) - scalars)
    for number, (dims, index) in blocks.items():
        specs[number] = pl.BlockSpec(dims, functools.partial(lambda place, step: place, index), memory_space=pltpu.VMEM)
    many = isinstance(outs, list)
    return pl.pallas_call(
        kernel,
        grid=(1,),
        out_shape=outs,
        in_specs=specs,
        out_specs=[vmem] * (len(outs) - scalar_outs) + [smem] * scalar_outs if many else vmem,
        scratch_shapes=list(scratch),
        compiler_params=pltpu.CompilerParams(vmem_limit_bytes=vmem_bytes),
        cost_estimate=pl.CostEstimate(flops=flops, bytes_accessed=2 * 2**20, transcendentals=0),
        name=name,
    )(*args)


def shape(*dims, dtype=bf16):
    return jax.ShapeDtypeStruct(dims, dtype)


def exchange(message):
    width = message.shape[1]
    blocks = message.reshape(PEERS, ROWS // PEERS, width)
    return lax.all_to_all(blocks, "pts", split_axis=0, concat_axis=0, tiled=True).reshape(ROWS, width)


def swap(array):
    return lax.ppermute(array, "grp", [(0, 1), (1, 0)])


SLOTS = ((ROWS, 384), (0, 0))
LABELS = ((ROWS, 128), (0, 3))
PART = shape(PATCH, HALF)


def attend(number, core, own, other, gain, bias, qkv_own, qkv_other, proj_own, proj_other):
    qkv_block = ((None, 3, FULL, HALF), (number, 0, 0, 0))
    proj_block = ((None, HALF, FULL), (number, 0, 0))
    kept, sent = call(
        functools.partial(attention_kernel, block=number), "attention", [PART, PART],
        core, own, other, gain, bias, qkv_own, qkv_other, proj_own, proj_other,
        scalars=1, blocks={5: qkv_block, 6: qkv_block, 7: proj_block, 8: proj_block},
        scratch=[pltpu.VMEM((HEADS, PATCH, 128), bf16)] + [pltpu.VMEM((FULL, PATCH), bf16)] * 4
        + [pltpu.VMEM((PATCH, PATCH), f32)] * 4, flops=2 * 10**10,
    )
    return kept, swap(sent)


def local(features, hilbert_rank, trans_rank, ln_gain, ln_bias, w_qkv, w_proj):
    core = lax.axis_index("grp").astype(jnp.int32)
    mine, theirs = (core * PATCH).reshape(1), ((1 - core) * PATCH).reshape(1)
    core = core.reshape(1)
    qkv = w_qkv.transpose(0, 2, 1, 3)
    weights = (ln_gain, ln_bias, qkv, swap(qkv), w_proj, swap(w_proj))
    message, index = call(
        send_kernel, "send", [shape(ROWS, 512), shape(8, ROWS, dtype=jnp.int32)],
        hilbert_rank.reshape(1, ROWS), trans_rank.reshape(1, ROWS), features, vmem_bytes=MOST_VMEM,
    )
    arrived = exchange(message)
    ranks, table = shape(8, PATCH, dtype=f32), shape(8, ROWS, dtype=jnp.int32)
    columns = pltpu.VMEM((ROWS, 128), jnp.int32)
    leaving, other_ranks, codes = call(
        decode_place_kernel, "place_other", [PART, ranks, table], theirs, arrived, arrived, scalars=1,
        blocks={1: SLOTS, 2: LABELS},
    )
    other = swap(leaving)
    own, own_ranks = call(
        place_kernel, "place_own", [PART, ranks], mine, arrived, codes, scalars=1, blocks={1: SLOTS}
    )
    kept, received = attend(0, core, own, other, *weights)
    leave, most = call(
        leave_kernel, "leave", [table, shape(1, 128, dtype=f32)], core, own_ranks, other_ranks, scalars=1,
        scratch=[columns],
    )
    message = exchange(
        call(direct_kernel, "direct", shape(ROWS, 768), core, kept, received, leave, most, scalars=1)
    )
    arrive = call(arrive_kernel, "arrive", table, codes, scratch=[pltpu.VMEM((ROWS, 128), f32)])
    leaving, full = call(
        place_direct_kernel, "direct_other", [PART, shape(1, 1, dtype=jnp.int32)], theirs, arrive, message, scalars=1,
        scalar_outs=1,
    )
    other = swap(leaving)
    own = call(place_direct_kernel, "direct_own", PART, mine, arrive, message, scalars=1)

    def by_home(own, other):
        message = exchange(call(
            slow_return_kernel, "slow_return", shape(ROWS, 384), core, kept, received, codes, scalars=1,
            scratch=[columns],
        ))
        message = exchange(call(
            slow_middle_kernel, "slow_middle", shape(ROWS, 384), index, message,
            scratch=[columns, pltpu.VMEM((ROWS, HALF), bf16)],
        ))
        rows = call(slow_place_kernel, "slow_place", shape(ROWS, HALF), message, codes)
        leaving = lax.dynamic_slice_in_dim(rows, theirs[0], PATCH)
        return lax.dynamic_slice_in_dim(rows, mine[0], PATCH), swap(leaving)

    own, other = lax.cond(full[0, 0] > 0, by_home, lambda own, other: (own, other), own, other)
    kept, received = attend(1, core, own, other, *weights)
    landed = exchange(call(return_kernel, "return", shape(ROWS, 384), core, kept, received, codes, scalars=1))
    return call(home_kernel, "home", shape(ROWS, HALF), index, landed)


def solution(mesh):
    in_specs = (
        P("pts", "grp"),
        P("pts"),
        P("pts"),
        P(),
        P(),
        P(None, None, None, "grp"),
        P(None, "grp", None),
    )
    return jax.shard_map(local, mesh=mesh, in_specs=in_specs, out_specs=P("pts", "grp"), check_vma=False)
```

```python
import functools
import math

import jax
import jax.numpy as jnp
from jax import lax
from jax.experimental import pallas as pl
from jax.experimental.pallas import tpu as pltpu
from jax.sharding import PartitionSpec as P

ROWS = 1024
PEERS = 128
HALF = 256
FULL = 512
PATCH = 512
HEADS = 32
HEAD = 16
EPSILON = 1e-05
EXP_SCALE = HEAD ** (-0.5) * math.log2(math.e)
CHUNK = 128
SLOW = 32
VMEM_BYTES = 24 * 2**20
MOST_VMEM = 60 * 2**20

DIRECT = 24


f32 = jnp.float32
bf16 = jnp.bfloat16


def iota(shape, axis):
    return lax.broadcasted_iota(jnp.int32, shape, axis)


def dot(left, right):
    return jnp.dot(left, right, preferred_element_type=f32)


def onehot(mask):
    return jnp.where(mask, 1.0, 0.0).astype(bf16)


def integers(array):
    return array.astype(jnp.int32)


def earlier_peers(owner, earlier):
    owners = onehot(iota((PEERS, ROWS), 0) == owner)
    running = dot(owners, earlier)
    return owners, integers(jnp.sum(running * owners.astype(f32), axis=0, keepdims=True))


def before():
    return onehot(iota((ROWS, ROWS), 0) < iota((ROWS, ROWS), 1))


def pack(low_mask, high_mask, rows, out_ref, to=slice(None)):
    out_ref[to, :HALF] = dot(onehot(low_mask), rows).astype(bf16)
    high = dot(onehot(high_mask), rows)
    first = (iota((high.shape[0], 128), 0) & 4) == 0
    out_ref[to, HALF:384] = jnp.where(first, high[:, :128], high[:, 128:]).astype(bf16)


def tails(message):
    tail = message[:, HALF:384].astype(f32)
    return jnp.concatenate([tail.astype(bf16), pltpu.roll(tail, ROWS - 4, 0).astype(bf16)], axis=1)


def in_chunks(body, chunk):
    def step(number, carry):
        body(pl.multiple_of(number * chunk, chunk))
        return carry

    lax.fori_loop(0, ROWS // chunk, step, 0)


def transposed(rows):
    rows = rows.astype(f32)
    return jnp.concatenate([rows, jnp.zeros((128 - rows.shape[0], rows.shape[1]), f32)], axis=0).T


def send_kernel(hilbert_ref, trans_ref, features_ref, message_ref, index_ref):
    features = features_ref[...]
    earlier = before()
    ranks = [hilbert_ref[...], trans_ref[...]]
    owners = [lax.shift_right_logical(rank, 10) for rank in ranks]
    highs = [lax.shift_right_logical(rank, 5) & 31 for rank in ranks]
    lows = [rank & 31 for rank in ranks]
    values = [[highs[0] + 1, lows[0], owners[1], highs[1], lows[1]], [highs[1] + 1, lows[1], owners[0]]]
    steps = iota((16, ROWS), 0)
    labels = jnp.zeros((PEERS, 128), f32)
    index = []
    for order in range(2):
        peers, slot = earlier_peers(owners[order], earlier)
        index.append(jnp.where(slot < 8, owners[order] * 8 + slot, -1))
        index.append(jnp.where((slot >= 8) & (slot < 12), owners[order] * 8 + slot - 8, -1))
        here = steps == slot
        spread = jnp.concatenate(
            [jnp.where(here, value, 0).astype(f32).astype(bf16) for value in values[order]], axis=0
        )
        empty = [jnp.zeros((16 * (8 - len(values[order])), ROWS), bf16)]
        spread = jnp.concatenate([spread] + empty if order == 0 else empty + [spread], axis=0)
        labels += lax.dot_general(peers, spread, (((1,), (1,)), ((), ())), preferred_element_type=f32)
    index_ref[...] = jnp.concatenate(index + [jnp.full((4, ROWS), -1, jnp.int32)], axis=0)
    rows = iota((ROWS, ROWS), 0)
    pack(rows == index[0], (rows & ~4) == index[1], features, message_ref)
    labels = jnp.broadcast_to(labels[:, None, :], (PEERS, 8, 128)).reshape(ROWS, 128)
    message_ref[:, 384:] = labels.astype(bf16)


def decode(labels):
    labels = labels.astype(f32)
    row, lane = iota((ROWS, 128), 0), iota((ROWS, 128), 1)
    low = jnp.where((lane & 15) == (row & 7), labels, 0.0).astype(bf16)
    high = jnp.where((lane & 15) == 8 + (row & 3), labels, 0.0).astype(bf16)
    value, column = lax.shift_right_logical(iota((128, 128), 0), 4), iota((128, 128), 1)

    def table(entries):
        weights = jnp.zeros((128, 128), f32)
        for to, source, weight in entries:
            weights += jnp.where((column == to) & (value == source), float(weight), 0.0)
        return weights.astype(bf16)

    entries = [(0, 0, 32), (0, 1, 1), (2, 2, 1024), (2, 3, 32), (2, 4, 1), (4, 5, 32), (4, 6, 1), (6, 7, 1)]
    codes = dot(low, table(entries)) + dot(high, table([(to + 1, v, w) for to, v, w in entries]))
    codes = integers(codes.T[:8])
    kind = iota((8, ROWS), 0)
    return codes - jnp.where((kind < 2) | (kind == 4) | (kind == 5), 32, 0)


def position_masks(codes, order, targets):
    low, high = codes[4 * order:4 * order + 1], codes[4 * order + 1:4 * order + 2]
    return targets == low, targets == jnp.where((iota((1, ROWS), 1) & 4) == 0, high, -1)


def place_rows(base_ref, message_ref, codes, out_ref, ranks_ref):
    def parts(rank):
        device = lax.shift_right_logical(rank, 10)
        return transposed(jnp.concatenate([device, lax.shift_right_logical(rank, 5) & 31, rank & 31], axis=0))

    message = message_ref[...]
    low_mask, high_mask = position_masks(codes, 0, iota((PATCH, ROWS), 0) + base_ref[0])
    low = jnp.concatenate([message[:, :HALF], parts(codes[2:3]).astype(bf16)], axis=1)
    high = jnp.concatenate([tails(message), parts(codes[3:4]).astype(bf16)], axis=1)
    placed = dot(onehot(low_mask), low) + dot(onehot(high_mask), high)
    out_ref[...] = placed[:, :HALF].astype(bf16)
    ranks_ref[...] = placed[:, HALF:].T[:8]


def decode_place_kernel(base_ref, message_ref, labels_ref, out_ref, ranks_ref, codes_ref):
    codes = decode(labels_ref[...])
    codes_ref[...] = codes
    place_rows(base_ref, message_ref, codes, out_ref, ranks_ref)


def place_kernel(base_ref, message_ref, codes_ref, out_ref, ranks_ref):
    place_rows(base_ref, message_ref, codes_ref[...], out_ref, ranks_ref)


def in_order(core_ref, own, other, axis=0):
    first = core_ref[0] == 0
    return jnp.concatenate([jnp.where(first, own, other), jnp.where(first, other, own)], axis=axis)


def return_kernel(core_ref, kept_ref, received_ref, codes_ref, out_ref):
    rows = in_order(core_ref, kept_ref[...], received_ref[...])
    codes = integers(transposed(codes_ref[4:6, :]))
    targets = iota((ROWS, ROWS), 1)
    pack(targets == codes[:, 0:1], targets == codes[:, 1:2], rows, out_ref)


def home_kernel(index_ref, message_ref, out_ref):
    message = message_ref[...]
    columns = integers(transposed(index_ref[2:4, :]))
    sources = iota((ROWS, ROWS), 1)
    placed = dot(onehot(sources == columns[:, 0:1]), message[:, :HALF])
    placed += dot(onehot(sources == columns[:, 1:2]), tails(message))
    out_ref[...] = placed.astype(bf16)


def slow_return_kernel(core_ref, kept_ref, received_ref, codes_ref, out_ref, columns_s):
    rows = in_order(core_ref, kept_ref[...], received_ref[...])
    columns_s[...] = integers(transposed(codes_ref[0:2, :]))

    def some(start):
        columns = columns_s[pl.ds(start, SLOW), :]
        targets = iota((SLOW, ROWS), 1)
        pack(targets == columns[:, 0:1], targets == columns[:, 1:2], rows, out_ref, pl.ds(start, SLOW))

    in_chunks(some, SLOW)


def slow_middle_kernel(index_ref, message_ref, out_ref, columns_s, rows_s):
    message = message_ref[...]
    tail = tails(message)
    columns_s[...] = integers(transposed(index_ref[0:2, :]))
    low, high = index_ref[2:3, :], index_ref[3:4, :]

    def home(start):
        columns = columns_s[pl.ds(start, SLOW), :]
        sources = iota((SLOW, ROWS), 1)
        placed = dot(onehot(sources == columns[:, 0:1]), message[:, :HALF])
        rows_s[pl.ds(start, SLOW), :] = (placed + dot(onehot(sources == columns[:, 1:2]), tail)).astype(bf16)

    def leave(start):
        targets = iota((SLOW, ROWS), 0) + start
        pack(targets == low, (targets & ~4) == high, rows_s[...], out_ref, pl.ds(start, SLOW))

    in_chunks(home, SLOW)
    in_chunks(leave, SLOW)


def slow_place_kernel(message_ref, codes_ref, out_ref):
    message, codes = message_ref[...], codes_ref[...]
    tail = tails(message)

    def some(start):
        low, high = position_masks(codes, 1, iota((SLOW, ROWS), 0) + start)
        placed = dot(onehot(low), message[:, :HALF]) + dot(onehot(high), tail)
        out_ref[pl.ds(start, SLOW), :] = placed.astype(bf16)

    in_chunks(some, SLOW)


def direct_index(owner, slot):
    row, third = owner * 8 + (slot & 7), lax.shift_right_logical(slot, 3)
    return jnp.where(iota((8, ROWS), 0) == third, row, -1)


def leave_kernel(core_ref, own_ref, other_ref, index_ref, most_ref, ranks_s):
    parts = integers(in_order(core_ref, own_ref[...], other_ref[...], axis=1))
    owner = parts[0:1]
    rank = owner * 1024 + parts[1:2] * 32 + parts[2:3]
    ranks_s[...] = integers(transposed(rank))
    ahead = jnp.zeros((8, ROWS), f32)
    for start in range(0, ROWS, 512):
        column = ranks_s[start:start + 512, 0:1]
        here = jnp.where((column >= owner * 1024) & (column < rank), 1.0, 0.0)
        ahead = ahead + jnp.sum(here.reshape(64, 8, ROWS), axis=0)
    slot = integers(jnp.sum(ahead, axis=0, keepdims=True))
    index_ref[...] = direct_index(owner, slot)
    most_ref[...] = jnp.broadcast_to(jnp.max(slot.astype(f32), axis=1, keepdims=True) + 1.0, (1, 128))


def direct_kernel(core_ref, kept_ref, received_ref, index_ref, most_ref, out_ref):
    rows = in_order(core_ref, kept_ref[...], received_ref[...])
    targets = iota((ROWS, ROWS), 0)
    for third in range(DIRECT // 8):
        columns = slice(third * HALF, (third + 1) * HALF)
        packed = dot(onehot(targets == index_ref[third:third + 1]), rows)
        if third == 0:
            packed = jnp.where(most_ref[:, :1] > DIRECT, jnp.inf, packed)
        out_ref[:, columns] = packed.astype(bf16)


def arrive_kernel(codes_ref, index_ref, owners_s):
    codes = codes_ref[...]
    low_owner = transposed(codes[6:7]).astype(bf16)
    high_owner = transposed(codes[7:8]).astype(bf16)

    def some(start):
        low, high = position_masks(codes, 1, iota((64, ROWS), 0) + start)
        owners_s[pl.ds(start, 64), :] = dot(onehot(low), low_owner) + dot(onehot(high), high_owner)

    in_chunks(some, 64)
    owner = integers(owners_s[...].T[0:1])
    _, slot = earlier_peers(owner, before())
    index_ref[...] = direct_index(owner, slot)


def place_direct_kernel(base_ref, index_ref, message_ref, out_ref, *full_ref):
    if full_ref:
        largest = jnp.max(jnp.abs(message_ref[:, :128].astype(f32)))
        full_ref[0][0, 0] = jnp.where(largest == jnp.inf, 1, 0)
    index = index_ref[0:3, :]
    index = integers(transposed(jnp.where(base_ref[0] == 0, index[:, :PATCH], index[:, PATCH:])))
    sources = iota((PATCH, ROWS), 1)
    placed = jnp.zeros((PATCH, HALF), f32)
    for third in range(DIRECT // 8):
        mask = sources == index[:, third:third + 1]
        placed += dot(onehot(mask), message_ref[:, third * HALF:(third + 1) * HALF])
    out_ref[...] = placed.astype(bf16)


def attention_kernel(
    core_ref, own_ref, other_ref, gain_ref, bias_ref, qkv_own_ref, qkv_other_ref, proj_own_ref, proj_other_ref,
    kept_ref, sent_ref, keys_s, queries_s, values_s, attended_s, weights_s, scores_a, scores_b, exponent_a, exponent_b, *, block,
):
    first = core_ref[0] == 0
    own, other = own_ref[...], other_ref[...]
    ordered = jnp.concatenate([jnp.where(first, own, other), jnp.where(first, other, own)], axis=1)
    ordered = ordered.astype(f32)
    average = jnp.sum(ordered, axis=1, keepdims=True) / FULL
    variance = jnp.sum(ordered * ordered, axis=1, keepdims=True) / FULL - average * average
    normed = (ordered - average) * lax.rsqrt(variance + EPSILON) * gain_ref[block:block + 1] + bias_ref[block:block + 1]
    normed = normed.astype(bf16)
    lane = iota((PATCH, 128), 1)
    for part, weight_ref in enumerate((qkv_own_ref, qkv_other_ref)):
        channels = slice(part * HALF, (part + 1) * HALF)
        queries_s[channels, :] = dot(normed, weight_ref[0]).T.astype(bf16)
        values_s[channels, :] = dot(normed, weight_ref[2]).T.astype(bf16)
        keys = dot(normed, weight_ref[1]).astype(bf16)
        for group in range(2):
            keys_g = keys[:, group * 128:(group + 1) * 128]
            for head in range(8):
                keys_s[part * 16 + group * 8 + head] = jnp.where(lane >> 4 == head, keys_g, jnp.zeros_like(keys_g))

    def channels_of(head):
        return pl.ds(pl.multiple_of(head * HEAD, HEAD), HEAD)

    def fold(array, reduction):
        return reduction(array.reshape(array.shape[0] // 8, 8, array.shape[1]), axis=0)

    def stage(scoring, exping, mixing, scores_to, scores_from, exponent_to, exponent_from, row_max, total):
        inverse = 1.0 / total
        new_max = jnp.full((8, PATCH), -jnp.inf, f32)
        new_total = jnp.zeros((8, PATCH), f32)
        attended = jnp.zeros((HEAD, PATCH), f32)
        for start in range(0, PATCH, CHUNK):
            part = slice(start, start + CHUNK)
            if scoring is not None:
                group = pl.ds(pl.multiple_of((scoring >> 3) * 128, 128), 128)
                scores = dot(keys_s[scoring, part, :], queries_s[group, :])
                scores_to[part, :] = scores
                new_max = jnp.maximum(new_max, fold(scores, jnp.max))
            if mixing is not None:
                weights_s[part, :] = (exponent_from[part, :] * inverse).astype(bf16)
            if exping is not None:
                exponent = jnp.exp2((scores_from[part, :] - row_max) * EXP_SCALE)
                exponent_to[part, :] = exponent
                new_total = new_total + fold(exponent, jnp.sum)
            if mixing is not None and start % (2 * CHUNK) == CHUNK:
                both = slice(start - CHUNK, start + CHUNK)
                attended = attended + dot(values_s[channels_of(mixing), both], weights_s[both, :])
        if mixing is not None:
            attended_s[channels_of(mixing), :] = attended.astype(bf16)
        return jnp.max(new_max, axis=0, keepdims=True), jnp.sum(new_total, axis=0, keepdims=True)

    def two_stages(step, carry):
        head = 2 * step
        carry = stage(head + 2, head + 1, head, scores_a, scores_b, exponent_b, exponent_a, *carry)
        return stage(head + 3, head + 2, head + 1, scores_b, scores_a, exponent_a, exponent_b, *carry)

    one = jnp.ones((1, PATCH), f32)
    row_max, _ = stage(0, None, None, scores_a, None, None, None, one, one)
    carry = stage(1, 0, None, scores_b, scores_a, exponent_a, None, row_max, one)
    carry = lax.fori_loop(0, HEADS // 2 - 1, two_stages, carry)
    carry = stage(None, HEADS - 1, HEADS - 2, None, scores_b, exponent_b, exponent_a, *carry)
    stage(None, None, HEADS - 1, None, None, None, exponent_b, one, carry[1])
    attended = attended_s[...].astype(f32).T.astype(bf16)
    mixture = dot(attended[:, :HALF], proj_own_ref[...]) + dot(attended[:, HALF:], proj_other_ref[...])
    updated = (ordered + mixture).astype(bf16)
    kept_ref[...] = jnp.where(first, updated[:, :HALF], updated[:, HALF:])
    sent_ref[...] = jnp.where(first, updated[:, HALF:], updated[:, :HALF])


def call(kernel, name, outs, *args, scalars=0, scalar_outs=0, blocks={}, scratch=(), flops=10**9, vmem_bytes=VMEM_BYTES):
    vmem = pl.BlockSpec(memory_space=pltpu.VMEM)
    smem = pl.BlockSpec(memory_space=pltpu.SMEM)
    specs = [smem] * scalars + [vmem] * (len(args) - scalars)
    for number, (dims, index) in blocks.items():
        specs[number] = pl.BlockSpec(dims, functools.partial(lambda place, step: place, index), memory_space=pltpu.VMEM)
    many = isinstance(outs, list)
    return pl.pallas_call(
        kernel,
        grid=(1,),
        out_shape=outs,
        in_specs=specs,
        out_specs=[vmem] * (len(outs) - scalar_outs) + [smem] * scalar_outs if many else vmem,
        scratch_shapes=list(scratch),
        compiler_params=pltpu.CompilerParams(vmem_limit_bytes=vmem_bytes),
        cost_estimate=pl.CostEstimate(flops=flops, bytes_accessed=2 * 2**20, transcendentals=0),
        name=name,
    )(*args)


def shape(*dims, dtype=bf16):
    return jax.ShapeDtypeStruct(dims, dtype)


def exchange(message):
    width = message.shape[1]
    blocks = message.reshape(PEERS, ROWS // PEERS, width)
    return lax.all_to_all(blocks, "pts", split_axis=0, concat_axis=0, tiled=True).reshape(ROWS, width)


def swap(array):
    return lax.ppermute(array, "grp", [(0, 1), (1, 0)])


SLOTS = ((ROWS, 384), (0, 0))
LABELS = ((ROWS, 128), (0, 3))
PART = shape(PATCH, HALF)


def attend(number, core, own, other, gain, bias, qkv_own, qkv_other, proj_own, proj_other):
    qkv_block = ((None, 3, FULL, HALF), (number, 0, 0, 0))
    proj_block = ((None, HALF, FULL), (number, 0, 0))
    kept, sent = call(
        functools.partial(attention_kernel, block=number), "attention", [PART, PART],
        core, own, other, gain, bias, qkv_own, qkv_other, proj_own, proj_other,
        scalars=1, blocks={5: qkv_block, 6: qkv_block, 7: proj_block, 8: proj_block},
        scratch=[pltpu.VMEM((HEADS, PATCH, 128), bf16)] + [pltpu.VMEM((FULL, PATCH), bf16)] * 4
        + [pltpu.VMEM((PATCH, PATCH), f32)] * 4, flops=2 * 10**10,
    )
    return kept, swap(sent)


def local(features, hilbert_rank, trans_rank, ln_gain, ln_bias, w_qkv, w_proj):
    core = lax.axis_index("grp").astype(jnp.int32)
    mine, theirs = (core * PATCH).reshape(1), ((1 - core) * PATCH).reshape(1)
    core = core.reshape(1)
    qkv = w_qkv.transpose(0, 2, 1, 3)
    weights = (ln_gain, ln_bias, qkv, swap(qkv), w_proj, swap(w_proj))
    message, index = call(
        send_kernel, "send", [shape(ROWS, 512), shape(8, ROWS, dtype=jnp.int32)],
        hilbert_rank.reshape(1, ROWS), trans_rank.reshape(1, ROWS), features, vmem_bytes=MOST_VMEM,
    )
    arrived = exchange(message)
    ranks, table = shape(8, PATCH, dtype=f32), shape(8, ROWS, dtype=jnp.int32)
    columns = pltpu.VMEM((ROWS, 128), jnp.int32)
    leaving, other_ranks, codes = call(
        decode_place_kernel, "place_other", [PART, ranks, table], theirs, arrived, arrived, scalars=1,
        blocks={1: SLOTS, 2: LABELS},
    )
    other = swap(leaving)
    own, own_ranks = call(
        place_kernel, "place_own", [PART, ranks], mine, arrived, codes, scalars=1, blocks={1: SLOTS}
    )
    kept, received = attend(0, core, own, other, *weights)
    leave, most = call(
        leave_kernel, "leave", [table, shape(1, 128, dtype=f32)], core, own_ranks, other_ranks, scalars=1,
        scratch=[columns],
    )
    message = exchange(
        call(direct_kernel, "direct", shape(ROWS, 768), core, kept, received, leave, most, scalars=1)
    )
    arrive = call(arrive_kernel, "arrive", table, codes, scratch=[pltpu.VMEM((ROWS, 128), f32)])
    leaving, full = call(
        place_direct_kernel, "direct_other", [PART, shape(1, 1, dtype=jnp.int32)], theirs, arrive, message, scalars=1,
        scalar_outs=1,
    )
    other = swap(leaving)
    own = call(place_direct_kernel, "direct_own", PART, mine, arrive, message, scalars=1)

    def by_home(own, other):
        message = exchange(call(
            slow_return_kernel, "slow_return", shape(ROWS, 384), core, kept, received, codes, scalars=1,
            scratch=[columns],
        ))
        message = exchange(call(
            slow_middle_kernel, "slow_middle", shape(ROWS, 384), index, message,
            scratch=[columns, pltpu.VMEM((ROWS, HALF), bf16)],
        ))
        rows = call(slow_place_kernel, "slow_place", shape(ROWS, HALF), message, codes)
        leaving = lax.dynamic_slice_in_dim(rows, theirs[0], PATCH)
        return lax.dynamic_slice_in_dim(rows, mine[0], PATCH), swap(leaving)

    own, other = lax.cond(full[0, 0] > 0, by_home, lambda own, other: (own, other), own, other)
    kept, received = attend(1, core, own, other, *weights)
    landed = exchange(call(return_kernel, "return", shape(ROWS, 384), core, kept, received, codes, scalars=1))
    return call(home_kernel, "home", shape(ROWS, HALF), index, landed)


def solution(mesh):
    in_specs = (
        P("pts", "grp"),
        P("pts"),
        P("pts"),
        P(),
        P(),
        P(None, None, None, "grp"),
        P(None, "grp", None),
    )
    return jax.shard_map(local, mesh=mesh, in_specs=in_specs, out_specs=P("pts", "grp"), check_vma=False)
```
